1024 devices in a mesh: dp: 16 (over z), expert: 64 (over y, x, core).
Axes of the slice: x: 4, y: 8, z: 16, core: 2. Of those that a mesh axis runs over, the one named last changes fastest.
Arguments:
- activations: bfloat16 [2, 49152, 1024], P(None, ('dp', 'expert')), may hold values from -6 to 6
- out_grads: bfloat16 [2, 49152, 1024], P(None, ('dp', 'expert')), may hold values from -6 to 6
- chosen_ids: int32 [2, 16, 64, 96], P(None, 'dp', 'expert'), may hold values from 0 to 3071, as said below
- gate_logits: int32 [2, 16, 64, 96], P(None, 'dp', 'expert'), may hold values from -16384 to 16384
- w_gate: bfloat16 [64, 1024, 768], P('expert'), may hold values from -0.1875 to 0.1875
- w_up: bfloat16 [64, 1024, 768], P('expert'), may hold values from -0.1875 to 0.1875
- w_down: bfloat16 [64, 768, 1024], P('expert'), may hold values from -0.21875 to 0.21875
Outputs:
- token_grads: bfloat16 [2, 49152, 1024], P(None, ('dp', 'expert'))
- gate_wgrad: bfloat16 [64, 1024, 768], P('expert', 'dp')
- up_wgrad: bfloat16 [64, 1024, 768], P('expert', 'dp')
- down_wgrad: bfloat16 [64, 768, 1024], P('expert', 'dp')
The draws below stay inside these ranges and needn't reach their ends.
Inputs may be any that keep to these rules, and one draw needn't show every extreme that they name: `chosen_ids`: each expert's 96 entries for one micro-batch and data group are distinct. At most 2 of them fall in one device's aligned block of 48 tokens, and in every list some block holds exactly 2.
All inputs are finite; a program needn't handle non-finite values.
Results may differ from the reference program's by a relative error of at most 0.023.
Values may be sent and summed in bfloat16 or wider, within the bound.
A program may use at most 32 MiB of HBM per device.

```python
import math
import jax
import jax.numpy as jnp
from jax import lax

D = 1024
F = 768
MICRO = 2
TOK_DEV = 48
EXPERTS = 64
GROUPS = 16
GROUP_TOK = 3072
TOKENS = 49152
CAP = 96
MOST = 2


def choose_list(key):
    first, second, third, fourth = jax.random.split(key, 4)
    cells = EXPERTS * MOST
    favored = jax.random.randint(first, (), 0, EXPERTS)
    shuffled = jax.random.permutation(second, cells)
    holders = shuffled // MOST
    priority = jnp.where(holders == favored, 0, 1).astype(jnp.int32)
    ranked = shuffled[jnp.argsort(priority, stable=True)][:CAP]
    picks = jax.vmap(lambda inner: jax.random.permutation(inner, TOK_DEV)[:MOST])(jax.random.split(third, EXPERTS))
    holder = ranked // MOST
    column = ranked - holder * MOST
    tokens = holder * TOK_DEV + picks[holder, column]
    return tokens[jax.random.permutation(fourth, CAP)].astype(jnp.int32)


def draw_chosen_ids(key, part):
    key = jax.random.fold_in(key, 7)
    keys = jax.random.split(key, MICRO * GROUPS * EXPERTS)
    lists = jax.vmap(choose_list)(keys)
    return lists.reshape(MICRO, GROUPS, EXPERTS, CAP)


def plant(array, key, least, top_value):
    longest = array.shape.index(max(array.shape))
    spots = []
    for shift in (0, 1):
        where = [jax.random.randint(jax.random.fold_in(key, axis), (), 0, length) for axis, length in enumerate(array.shape)]
        where[longest] = (where[longest] + shift) % array.shape[longest]
        spots.append(tuple(where))
    return array.at[spots[0]].set(least).at[spots[1]].set(top_value)


def levels(rng, shape, pieces, smallest, top_value):
    def one(axis_at, parts):
        steps = jax.random.uniform(jax.random.fold_in(jax.random.fold_in(rng, 6), axis_at), (parts,), jnp.float32, smallest / len(pieces), top_value / len(pieces))
        return jnp.repeat(jnp.exp(steps), shape[axis_at] // parts).reshape((-1,) + (1,) * (len(shape) - axis_at - 1))

    gain = one(*pieces[0])
    for cut in pieces[1:]:
        gain = gain * one(*cut)
    return gain


def noise(stream_key, extent, width, most, pieces=(), held_as=jnp.bfloat16):
    array = width * jax.random.normal(stream_key, extent, jnp.float32)
    if pieces:
        array = array * levels(stream_key, extent, pieces, -0.22, 0.18)
    return jnp.clip(array, -most, most).astype(held_as)


def setup_inputs(seed: int = 0) -> dict:
    arg_keys = jax.random.split(jax.random.key(seed), 8)
    activations = noise(arg_keys[0], (MICRO, TOKENS, D), 1.0, 6.0, ((1, 1024),))
    out_grads = noise(arg_keys[1], (MICRO, TOKENS, D), 1.0, 6.0, ((1, 1024),))
    chosen_ids = draw_chosen_ids(jax.random.fold_in(arg_keys[7], 71), 0)
    gate_logits = plant(jax.random.randint(arg_keys[3], (MICRO, GROUPS, EXPERTS, CAP), -16384, 16385), jax.random.fold_in(arg_keys[3], 1), -16384, 16384).astype(jnp.int32)
    w_gate = noise(arg_keys[4], (EXPERTS, D, F), D ** -0.5, 0.1875, ((0, 64),))
    w_up = noise(arg_keys[5], (EXPERTS, D, F), D ** -0.5, 0.1875, ((0, 64),))
    w_down = noise(arg_keys[6], (EXPERTS, F, D), F ** -0.5, 0.21875, ((0, 64),))
    return dict(activations=activations, out_grads=out_grads, chosen_ids=chosen_ids, gate_logits=gate_logits, w_gate=w_gate, w_up=w_up, w_down=w_down)


def rounded(values):
    return lax.optimization_barrier(values.astype(jnp.bfloat16)).astype(jnp.float32)

def reference(activations, out_grads, chosen_ids, gate_logits, w_gate, w_up, w_down):
    inputs4 = activations.reshape(MICRO, GROUPS, GROUP_TOK, D)
    grads4 = out_grads.reshape(MICRO, GROUPS, GROUP_TOK, D)
    factor = 1.0 / math.sqrt(GROUPS * MICRO * CAP)
    picker = jax.vmap(jax.vmap(lambda table, index: table[index]))
    micro_index = lax.broadcasted_iota(jnp.int32, (MICRO, GROUPS, CAP), 0)
    group_index = lax.broadcasted_iota(jnp.int32, (MICRO, GROUPS, CAP), 1)
    contract = (((1,), (1,)), ((), ()))

    def group_sum(left, right):
        left4 = left.reshape(MICRO, GROUPS, CAP, -1).astype(jnp.float32)
        right4 = right.reshape(MICRO, GROUPS, CAP, -1).astype(jnp.float32)
        partial_sums = jnp.einsum('mgci,mgcj->gij', left4, right4, precision=lax.Precision.HIGHEST) * factor
        return lax.optimization_barrier(jnp.sum(rounded(partial_sums), axis=0)).astype(jnp.bfloat16)

    def expert_step(total, packed):
        chosen, logits, gate_mat, up_mat, down_mat = packed
        picked_x = picker(inputs4, chosen).reshape(-1, D)
        picked_g = picker(grads4, chosen).reshape(-1, D)
        gates = jax.nn.sigmoid(logits.astype(jnp.float32) * (1.0 / 4096.0)).reshape(-1, 1)
        hidden_gate = jnp.dot(picked_x, gate_mat, preferred_element_type=jnp.float32)
        hidden_up = jnp.dot(picked_x, up_mat, preferred_element_type=jnp.float32)
        sigma = jax.nn.sigmoid(hidden_gate)
        act_rows = (hidden_gate * sigma * hidden_up).astype(jnp.bfloat16)
        dy_rows = (gates * picked_g.astype(jnp.float32)).astype(jnp.bfloat16)
        dact = lax.dot_general(dy_rows, down_mat, contract, preferred_element_type=jnp.float32)
        dh_up = (dact * hidden_gate * sigma).astype(jnp.bfloat16)
        dh_gate = (dact * hidden_up * sigma * (1.0 + hidden_gate * (1.0 - sigma))).astype(jnp.bfloat16)
        dx_rows = (lax.dot_general(dh_gate, gate_mat, contract, preferred_element_type=jnp.float32) + lax.dot_general(dh_up, up_mat, contract, preferred_element_type=jnp.float32)).astype(jnp.bfloat16)
        total = total.at[micro_index, group_index, chosen].add(dx_rows.reshape(MICRO, GROUPS, CAP, D).astype(jnp.float32))
        return (total, (group_sum(picked_x, dh_gate), group_sum(picked_x, dh_up), group_sum(act_rows, dy_rows)))
    chosen_t = jnp.transpose(chosen_ids, (2, 0, 1, 3))
    logits_t = jnp.transpose(gate_logits, (2, 0, 1, 3))
    start = jnp.zeros((MICRO, GROUPS, GROUP_TOK, D), jnp.float32)
    total, grads = lax.scan(expert_step, start, (chosen_t, logits_t, w_gate, w_up, w_down))
    token_grads = total.astype(jnp.bfloat16).reshape(MICRO, TOKENS, D)
    return (token_grads, grads[0], grads[1], grads[2])
```

```python
import functools
import math

import jax
import jax.numpy as jnp
from jax import lax
from jax.experimental import pallas as pl
from jax.experimental.pallas import tpu as pltpu
from jax.sharding import PartitionSpec as P

MESH = pl.DeviceIdType.MESH
BF16 = jnp.bfloat16
F32 = jnp.float32
contract_rows = (((0,), (0,)), ((), ()))
contract_cols = (((1,), (1,)), ((), ()))


def iota(shape, axis):
    return lax.broadcasted_iota(jnp.int32, shape, axis)


def fused(
    sizes,
    ids_ref, logits_ref, x_ref, g_ref, wg_hbm, wu_hbm, wd_hbm,
    tok_ref, gate_ref, up_ref, down_ref,
    ids_send, logits_pad, ids_all, ids_flat,
    wg, wu, wd,
    xcat, gcat, onehot, send_x, send_g, got_x, got_g,
    xs, xs_t, dy, act_t, coef1, coef3, dh1, dh3, gates,
    dx_cat, send_r, got_r,
    part_g, part_u, part_d0, part_d1,
    ring_g, ring_u, ring_d0, ring_d1,
    w_sem, ids_ssem, ids_rsem, fwd_ssem, fwd_rsem, own_sem, ret_ssem, ret_rsem,
    ring_ssem, ring_rsem,
):
    E, G, T, D, F, C = sizes
    Q = D // 4
    S = G // 2
    R4 = 4 * E
    BP = min(16, E)
    BR = BP * 16
    BO = BP * 4
    NB = E // BP
    factor = 1.0 / math.sqrt(G * 2 * C)
    me = lax.axis_index("expert")
    z = lax.axis_index("dp")
    z_right = lax.rem(z + 1, G)
    z_left = lax.rem(z + G - 1, G)

    weights = [
        pltpu.make_async_copy(src.at[0], dst, w_sem.at[k])
        for k, (src, dst) in enumerate(((wg_hbm, wg), (wu_hbm, wu), (wd_hbm, wd)))
    ]
    for copy in weights:
        copy.start()

    barrier = pltpu.get_barrier_semaphore()

    def greet(k, carry):
        pl.semaphore_signal(
            barrier, inc=1, device_id=(z, lax.rem(me + k, E)), device_id_type=MESH
        )
        return carry

    lax.fori_loop(1, E, greet, 0)
    for other in (z_right, z_left):
        pl.semaphore_signal(barrier, inc=1, device_id=(other, me), device_id_type=MESH)

    ids_send[...] = jnp.full(ids_send.shape, -1, jnp.int32)
    logits_pad[...] = jnp.zeros(logits_pad.shape, jnp.int32)
    for m in range(2):
        ids_send[m : m + 1, 0:C] = ids_ref[m, 0]
        logits_pad[m : m + 1, 0:C] = logits_ref[m, 0]
    ids_all[pl.ds(me, 1)] = ids_send[...][None]

    pl.semaphore_wait(barrier, E - 1 + 2)

    def send_ids(k, carry):
        pltpu.make_async_remote_copy(
            src_ref=ids_send,
            dst_ref=ids_all.at[me],
            send_sem=ids_ssem,
            recv_sem=ids_rsem,
            device_id=(z, lax.rem(me + k, E)),
            device_id_type=MESH,
        ).start()
        return carry

    lax.fori_loop(1, E, send_ids, 0)

    for m in range(2):
        for q in range(4):
            rows = pl.ds((q * 2 + m) * T, T)
            xcat[rows, :] = x_ref[m, :, q * Q : (q + 1) * Q]
            gcat[rows, :] = g_ref[m, :, q * Q : (q + 1) * Q]

    row = iota((R4, 128), 0)
    micro_row = (row // 2) % 2
    mine = jnp.where(micro_row == 0, ids_send[0:1, :], ids_send[1:2, :]).astype(F32)
    marks = jnp.where(micro_row == 0, logits_pad[0:1, :], logits_pad[1:2, :]).astype(F32)
    low = ((row // 4) * T).astype(F32)
    inside = (mine >= low) & (mine < low + float(T))
    first = jnp.min(jnp.where(inside, mine, 1e6), axis=1, keepdims=True)
    last = jnp.max(jnp.where(inside, mine, -1.0), axis=1, keepdims=True)
    pick = jnp.where(row % 2 == 0, first, last)
    logit = jnp.sum(jnp.where(inside & (mine == pick), marks, 0.0), axis=1, keepdims=True)
    gates[...] = jax.nn.sigmoid(logit * (1.0 / 4096.0))

    pltpu.make_async_copy(ids_all.at[pl.ds(0, E - 1)], ids_all.at[pl.ds(0, E - 1)], ids_rsem).wait()

    for e in range(E):
        for m in range(2):
            ids_flat[m, e : e + 1, :] = ids_all[e, m : m + 1, :]
    lane = iota((E, 128), 1)
    table = jnp.full((E, 128), -1.0, F32)
    base = (me * T).astype(F32)
    for m in range(2):
        local = ids_flat[m].astype(F32) - base
        inside = (local >= 0.0) & (local < float(T))
        first = jnp.min(jnp.where(inside, local, 1e6), axis=1, keepdims=True)
        last = jnp.max(jnp.where(inside, local, -1.0), axis=1, keepdims=True)
        first_ok = jnp.where(first < 1e5, first, -1.0)
        last_ok = jnp.where(last > first, last, -1.0)
        table = jnp.where(lane == 2 * m, first_ok, table)
        table = jnp.where(lane == 2 * m + 1, last_ok, table)
    table = table.astype(BF16)

    OB = min(128, E * 16)
    for blk in range(E * 16 // OB):
        rows = pl.ds(blk * OB, OB)
        spread = (
            (iota((OB, E), 0) + blk * OB) // 16 == iota((OB, E), 1)
        ).astype(F32).astype(BF16)
        values = jnp.dot(spread, table, preferred_element_type=F32)
        row = iota((OB, 128), 0)
        chosen = jnp.sum(
            jnp.where(iota((OB, 128), 1) == row % 4, values, 0.0), axis=1, keepdims=True
        )
        line = iota((OB, 1), 0)
        place = ((line // 4) % 4) * (2 * T) + ((line // 2) % 2) * T
        target = jnp.where(chosen < 0.0, -1.0, chosen + place.astype(F32))
        hot = (iota((OB, 8 * T), 1).astype(F32) == target).astype(F32).astype(BF16)
        onehot[rows, :] = hot
        send_x[rows, :] = jnp.dot(hot, xcat[...], preferred_element_type=F32).astype(BF16)

    def exchange(src, dst, ssem, rsem, osem):
        here = pl.ds(pl.multiple_of(me * 16, 16), 16)
        own = pltpu.make_async_copy(src.at[here], dst.at[here], osem)
        own.start()

        def one(k, carry):
            peer = lax.rem(me + k, E)
            pltpu.make_async_remote_copy(
                src_ref=src.at[pl.ds(pl.multiple_of(peer * 16, 16), 16)],
                dst_ref=dst.at[here],
                send_sem=ssem,
                recv_sem=rsem,
                device_id=(z, peer),
                device_id_type=MESH,
            ).start()
            return carry

        lax.fori_loop(1, E, one, 0)
        return own

    def arrived(dst, rsem, own):
        own.wait()
        whole = dst.at[pl.ds(0, (E - 1) * 16)]
        pltpu.make_async_copy(whole, whole, rsem).wait()

    own_x = exchange(send_x, got_x, fwd_ssem.at[0], fwd_rsem.at[0], own_sem.at[0])
    for blk in range(E * 16 // OB):
        rows = pl.ds(blk * OB, OB)
        send_g[rows, :] = jnp.dot(
            onehot[rows, :], gcat[...], preferred_element_type=F32
        ).astype(BF16)
    own_g = exchange(send_g, got_g, fwd_ssem.at[1], fwd_rsem.at[1], own_sem.at[1])

    r = iota((BR, BR), 0)
    c = iota((BR, BR), 1)
    perm = (
        c == ((r // 4) % BP) * 16 + (r // BO) * 4 + r % 4
    ).astype(F32).astype(BF16)
    perm_t = (
        r == ((c // 4) % BP) * 16 + (c // BO) * 4 + c % 4
    ).astype(F32).astype(BF16)

    for copy in weights:
        copy.wait()
    arrived(got_x, fwd_rsem.at[0], own_x)
    for blk in range(NB):
        moved = jnp.dot(perm, got_x[blk * BR : (blk + 1) * BR, :], preferred_element_type=F32)
        for q in range(4):
            xs[blk * BO : (blk + 1) * BO, q * Q : (q + 1) * Q] = moved[
                q * BO : (q + 1) * BO
            ].astype(BF16)
    FT = min(256, F)
    for ft in range(F // FT):
        cols = slice(ft * FT, (ft + 1) * FT)
        h1 = jnp.dot(xs[...], wg[:, cols], preferred_element_type=F32)
        h3 = jnp.dot(xs[...], wu[:, cols], preferred_element_type=F32)
        sig = jax.nn.sigmoid(h1)
        gated = h1 * sig
        act_t[cols, :] = (gated * h3).astype(BF16).T
        coef3[:, cols] = gated
        coef1[:, cols] = h3 * sig * (1.0 + h1 * (1.0 - sig))
    for q in range(4):
        xs_t[q * Q : (q + 1) * Q, :] = xs[:, q * Q : (q + 1) * Q].T

    arrived(got_g, fwd_rsem.at[1], own_g)
    for blk in range(NB):
        moved = jnp.dot(perm, got_g[blk * BR : (blk + 1) * BR, :], preferred_element_type=F32)
        scale = gates[blk * BO : (blk + 1) * BO, :]
        for q in range(4):
            dy[blk * BO : (blk + 1) * BO, q * Q : (q + 1) * Q] = (
                moved[q * BO : (q + 1) * BO] * scale
            ).astype(BF16)

    parts = (part_g, part_u, part_d0, part_d1)
    rings = (ring_g, ring_u, ring_d0, ring_d1)
    heights = (D // G, D // G, F // G, F // G)
    starts = ((0, 1, 0, 1), (1, 0, 1, 0))

    def piece(p, chunk):
        return pl.ds(pl.multiple_of(chunk * heights[p], heights[p]), heights[p])

    def forward(way, p, step, src):
        pltpu.make_async_remote_copy(
            src_ref=src,
            dst_ref=rings[p].at[way, step],
            send_sem=ring_ssem.at[way, p, step],
            recv_sem=ring_rsem.at[way, p, step],
            device_id=(z_right if way == 0 else z_left, me),
            device_id_type=MESH,
        ).start()

    def ring_copy(way, p, step):
        return pltpu.make_async_remote_copy(
            src_ref=rings[p].at[way, step],
            dst_ref=rings[p].at[way, step],
            send_sem=ring_ssem.at[way, p, step],
            recv_sem=ring_rsem.at[way, p, step],
            device_id=(z_right if way == 0 else z_left, me),
            device_id_type=MESH,
        )

    far = lax.rem(z + S, G)

    def begin(p):
        forward(starts[0][p], p, 0, parts[p].at[piece(p, far)])

    for ft in range(F // FT):
        rows = slice(ft * FT, (ft + 1) * FT)
        for half, part in ((0, part_d0), (1, part_d1)):
            part[rows, :] = (
                jnp.dot(
                    act_t[rows, :],
                    dy[:, half * (D // 2) : (half + 1) * (D // 2)],
                    preferred_element_type=F32,
                )
                * factor
            ).astype(BF16)
    begin(2)
    begin(3)
    for ft in range(F // FT):
        cols = slice(ft * FT, (ft + 1) * FT)
        dact = lax.dot_general(dy[...], wd[cols, :], contract_cols, preferred_element_type=F32)
        dh1[:, cols] = (dact * coef1[:, cols]).astype(BF16)
        dh3[:, cols] = (dact * coef3[:, cols]).astype(BF16)
    for p, part, dh in ((0, part_g, dh1), (1, part_u, dh3)):
        for q in range(4):
            rows = slice(q * Q, (q + 1) * Q)
            part[rows, :] = (
                jnp.dot(xs_t[rows, :], dh[...], preferred_element_type=F32) * factor
            ).astype(BF16)
        begin(p)

    def chunk_at(way, step):
        if way == 0:
            return lax.rem(z + S - step + G, G)
        return lax.rem(z + S + step, G)

    def pass_on(way, p, step):
        ring_copy(way, p, step - 1).wait_recv()
        held = rings[p].at[way, step - 1]
        held[...] = (
            held[...].astype(F32) + parts[p][piece(p, chunk_at(way, step)), :].astype(F32)
        ).astype(BF16)
        forward(way, p, step, held)

    order = ((0, 2), (1, 3), (0, 0), (1, 1), (0, 3), (1, 2), (0, 1), (1, 0))
    for way, p in order:
        if starts[way][p] == 1:
            forward(way, p, 1, parts[p].at[piece(p, chunk_at(way, 1))])
    for way, p in order:
        if starts[way][p] == 0:
            pass_on(way, p, 1)

    for q in range(4):
        rows = slice(q * Q, (q + 1) * Q)
        dx = (
            lax.dot_general(dh1[...], wg[rows, :], contract_cols, preferred_element_type=F32)
            + lax.dot_general(dh3[...], wu[rows, :], contract_cols, preferred_element_type=F32)
        ).astype(BF16)
        for blk in range(NB):
            dx_cat[blk * BR + q * BO : blk * BR + (q + 1) * BO, :] = dx[blk * BO : (blk + 1) * BO]
    for blk in range(NB):
        rows = slice(blk * BR, (blk + 1) * BR)
        send_r[rows, :] = jnp.dot(
            perm_t, dx_cat[rows, :], preferred_element_type=F32
        ).astype(BF16)
    own_r = exchange(send_r, got_r, ret_ssem, ret_rsem, own_sem.at[2])

    def ring_step(step, carry):
        for way, p in order:
            pass_on(way, p, step)
        return carry

    lax.fori_loop(2, S, ring_step, 0)

    arrived(got_r, ret_rsem, own_r)
    summed = lax.dot_general(onehot[...], got_r[...], contract_rows, preferred_element_type=F32)
    for m in range(2):
        for q in range(4):
            tok_ref[m, :, q * Q : (q + 1) * Q] = summed[
                (q * 2 + m) * T : (q * 2 + m + 1) * T
            ].astype(BF16)

    def finish(p):
        ring_copy(0, p, S - 1).wait_recv()
        ring_copy(1, p, S - 1).wait_recv()
        return (
            rings[p][0, S - 1].astype(F32)
            + rings[p][1, S - 1].astype(F32)
            + parts[p][piece(p, z), :].astype(F32)
        ).astype(BF16)

    down_ref[0, :, 0 : D // 2] = finish(2)
    down_ref[0, :, D // 2 : D] = finish(3)
    gate_ref[0] = finish(0)
    up_ref[0] = finish(1)

    pltpu.make_async_copy(ids_all.at[pl.ds(0, E - 1)], ids_all.at[pl.ds(0, E - 1)], ids_ssem).wait()
    for src, sem in ((send_x, fwd_ssem.at[0]), (send_g, fwd_ssem.at[1]), (send_r, ret_ssem)):
        whole = src.at[pl.ds(0, (E - 1) * 16)]
        pltpu.make_async_copy(whole, whole, sem).wait()
    for way in range(2):
        for p in range(4):
            for step in range(starts[way][p], S):
                ring_copy(way, p, step).wait_send()


def body(activations, out_grads, chosen_ids, gate_logits, w_gate, w_up, w_down):
    E = lax.axis_size("expert")
    G = lax.axis_size("dp")
    T, D = activations.shape[1:]
    F = w_gate.shape[-1]
    C = chosen_ids.shape[-1]
    Q, S, R4, R16 = D // 4, G // 2, 4 * E, 16 * E
    vmem = pl.BlockSpec(memory_space=pltpu.VMEM)
    anywhere = pl.BlockSpec(memory_space=pl.ANY)
    V = pltpu.VMEM
    dma = pltpu.SemaphoreType.DMA
    scratch = [
        V((2, 128), jnp.int32), V((2, 128), jnp.int32),
        V((E, 2, 128), jnp.int32), V((2, E, 128), jnp.int32),
        V((D, F), BF16), V((D, F), BF16), V((F, D), BF16),
        V((8 * T, Q), BF16), V((8 * T, Q), BF16), V((R16, 8 * T), BF16),
        V((R16, Q), BF16), V((R16, Q), BF16), V((R16, Q), BF16), V((R16, Q), BF16),
        V((R4, D), BF16), V((D, R4), BF16), V((R4, D), BF16), V((F, R4), BF16),
        V((R4, F), F32), V((R4, F), F32), V((R4, F), BF16), V((R4, F), BF16), V((R4, 1), F32),
        V((R16, Q), BF16), V((R16, Q), BF16), V((R16, Q), BF16),
        V((D, F), BF16), V((D, F), BF16), V((F, D // 2), BF16), V((F, D // 2), BF16),
        V((2, S, D // G, F), BF16), V((2, S, D // G, F), BF16),
        V((2, S, F // G, D // 2), BF16), V((2, S, F // G, D // 2), BF16),
        dma((3,)), dma, dma, dma((2,)), dma((2,)), dma((3,)), dma, dma,
        dma((2, 4, S)), dma((2, 4, S)),
    ]
    shape = jax.ShapeDtypeStruct
    return pl.pallas_call(
        functools.partial(fused, (E, G, T, D, F, C)),
        out_shape=(
            shape((2, T, D), BF16),
            shape((1, D // G, F), BF16),
            shape((1, D // G, F), BF16),
            shape((1, F // G, D), BF16),
        ),
        in_specs=[vmem, vmem, vmem, vmem, anywhere, anywhere, anywhere],
        out_specs=(vmem, vmem, vmem, vmem),
        scratch_shapes=scratch,
        compiler_params=pltpu.CompilerParams(
            collective_id=0, has_side_effects=True, vmem_limit_bytes=48 * 1024 * 1024
        ),
    )(chosen_ids, gate_logits, activations, out_grads, w_gate, w_up, w_down)


def solution(mesh):
    placed = (
        P(None, ("dp", "expert"), None),
        P(None, ("dp", "expert"), None),
        P(None, "dp", "expert", None),
        P(None, "dp", "expert", None),
        P("expert", None, None),
        P("expert", None, None),
        P("expert", None, None),
    )
    return jax.shard_map(
        body,
        mesh=mesh,
        in_specs=placed,
        out_specs=(
            P(None, ("dp", "expert"), None),
            P("expert", "dp", None),
            P("expert", "dp", None),
            P("expert", "dp", None),
        ),
        check_vma=False,
    )
```

```python
import functools
import math

import jax
import jax.numpy as jnp
from jax import lax
from jax.experimental import pallas as pl
from jax.experimental.pallas import tpu as pltpu
from jax.sharding import PartitionSpec as P

MESH = pl.DeviceIdType.MESH
BF16 = jnp.bfloat16
F32 = jnp.float32
contract_rows = (((0,), (0,)), ((), ()))
contract_cols = (((1,), (1,)), ((), ()))


def iota(shape, axis):
    return lax.broadcasted_iota(jnp.int32, shape, axis)


def fused(
    sizes,
    ids_hbm, logits_hbm, x_hbm, g_hbm, wg_hbm, wu_hbm, wd_hbm,
    tok_ref, gate_ref, up_ref, down_ref,
    ids_ref, logits_ref, ids_send, logits_pad, ids_all, ids_flat,
    wg, wu, wd,
    xcat, gcat, onehot, send_x, send_g, got_x, got_g, dacc,
    xs, xs_t, dy, act_t, coef1, coef3, dh1, dh3, gates,
    dx_cat, send_r, got_r,
    part_g, part_u, part_d0, part_d1,
    ring_g, ring_u, ring_d0, ring_d1,
    w_sem, in_sem, ids_ssem, ids_rsem, fwd_ssem, fwd_rsem, own_sem, ret_ssem, ret_rsem,
    ring_ssem, ring_rsem,
):
    E, G, T, D, F, C = sizes
    Q = D // 4
    S = G // 2
    R4 = 4 * E
    BP = min(16, E)
    BR = BP * 16
    BO = BP * 4
    NB = E // BP
    factor = 1.0 / math.sqrt(G * 2 * C)
    me = lax.axis_index("expert")
    z = lax.axis_index("dp")
    z_right = lax.rem(z + 1, G)
    z_left = lax.rem(z + G - 1, G)

    RW = min(8, E // 2)
    CW = E // RW
    row_at = me // RW
    col_at = lax.rem(me, RW)

    small = [
        pltpu.make_async_copy(src, dst, in_sem.at[k])
        for k, (src, dst) in enumerate(((ids_hbm, ids_ref), (logits_hbm, logits_ref)))
    ]
    for copy in small:
        copy.start()

    def row_mate(k):
        return row_at * RW + lax.rem(col_at + k, RW)

    def col_mate(k):
        return lax.rem(row_at + k, CW) * RW + col_at

    barrier = pltpu.get_barrier_semaphore()
    mates = [(z, row_mate(k)) for k in range(1, RW)] + [(z, col_mate(k)) for k in range(1, CW)]
    for other in mates + [(z_right, me), (z_left, me)]:
        pl.semaphore_signal(barrier, inc=1, device_id=other, device_id_type=MESH)

    for m in range(2):
        for q in range(4):
            rows = pl.ds((q * 2 + m) * T, T)
            pltpu.make_async_copy(
                x_hbm.at[m, :, pl.ds(q * Q, Q)], xcat.at[rows, :], in_sem.at[2]
            ).start()
            for half in range(2):
                pltpu.make_async_copy(
                    g_hbm.at[m, :, pl.ds(half * (D // 2) + q * (Q // 2), Q // 2)],
                    gcat.at[half, rows, :],
                    in_sem.at[3],
                ).start()
    weights = [
        pltpu.make_async_copy(src.at[0], dst, w_sem.at[k])
        for k, (src, dst) in enumerate(((wg_hbm, wg), (wu_hbm, wu), (wd_hbm, wd)))
    ]
    for copy in weights:
        copy.start()
    for copy in small:
        copy.wait()

    ids_send[...] = jnp.full(ids_send.shape, -1, jnp.int32)
    logits_pad[...] = jnp.zeros(logits_pad.shape, jnp.int32)
    for m in range(2):
        ids_send[m : m + 1, 0:C] = ids_ref[m, 0]
        logits_pad[m : m + 1, 0:C] = logits_ref[m, 0]
    ids_all[pl.ds(me, 1)] = ids_send[...][None]

    pl.semaphore_wait(barrier, RW - 1 + CW - 1 + 2)

    for k in range(1, RW):
        pltpu.make_async_remote_copy(
            src_ref=ids_send,
            dst_ref=ids_all.at[me],
            send_sem=ids_ssem.at[0],
            recv_sem=ids_rsem.at[0],
            device_id=(z, row_mate(k)),
            device_id_type=MESH,
        ).start()
    near = ids_all.at[pl.ds(0, max(RW - 1, 1))]
    if RW > 1:
        pltpu.make_async_copy(near, near, ids_rsem.at[0]).wait()
    ours = ids_all.at[pl.ds(row_at * RW, RW)]
    for k in range(1, CW):
        pltpu.make_async_remote_copy(
            src_ref=ours,
            dst_ref=ours,
            send_sem=ids_ssem.at[1],
            recv_sem=ids_rsem.at[1],
            device_id=(z, col_mate(k)),
            device_id_type=MESH,
        ).start()

    row = iota((R4, 128), 0)
    micro_row = (row // 2) % 2
    mine = jnp.where(micro_row == 0, ids_send[0:1, :], ids_send[1:2, :]).astype(F32)
    marks = jnp.where(micro_row == 0, logits_pad[0:1, :], logits_pad[1:2, :]).astype(F32)
    low = ((row // 4) * T).astype(F32)
    inside = (mine >= low) & (mine < low + float(T))
    first = jnp.min(jnp.where(inside, mine, 1e6), axis=1, keepdims=True)
    last = jnp.max(jnp.where(inside, mine, -1.0), axis=1, keepdims=True)
    pick = jnp.where(row % 2 == 0, first, last)
    logit = jnp.sum(jnp.where(inside & (mine == pick), marks, 0.0), axis=1, keepdims=True)
    gates[...] = jax.nn.sigmoid(logit * (1.0 / 4096.0))

    rest = ids_all.at[pl.ds(0, (CW - 1) * RW)]
    pltpu.make_async_copy(rest, rest, ids_rsem.at[1]).wait()

    for e in range(E):
        for m in range(2):
            ids_flat[m, e : e + 1, :] = ids_all[e, m : m + 1, :]
    lane = iota((E, 128), 1)
    table = jnp.full((E, 128), -1.0, F32)
    base = (me * T).astype(F32)
    for m in range(2):
        local = ids_flat[m].astype(F32) - base
        inside = (local >= 0.0) & (local < float(T))
        first = jnp.min(jnp.where(inside, local, 1e6), axis=1, keepdims=True)
        last = jnp.max(jnp.where(inside, local, -1.0), axis=1, keepdims=True)
        first_ok = jnp.where(first < 1e5, first, -1.0)
        last_ok = jnp.where(last > first, last, -1.0)
        table = jnp.where(lane == 2 * m, first_ok, table)
        table = jnp.where(lane == 2 * m + 1, last_ok, table)
    table = table.astype(BF16)

    OB = min(128, E * 16)
    pltpu.make_async_copy(xcat, xcat, in_sem.at[2]).wait()
    for blk in range(E * 16 // OB):
        rows = pl.ds(blk * OB, OB)
        spread = (
            (iota((OB, E), 0) + blk * OB) // 16 == iota((OB, E), 1)
        ).astype(F32).astype(BF16)
        values = jnp.dot(spread, table, preferred_element_type=F32)
        row = iota((OB, 128), 0)
        chosen = jnp.sum(
            jnp.where(iota((OB, 128), 1) == row % 4, values, 0.0), axis=1, keepdims=True
        )
        line = iota((OB, 1), 0)
        place = ((line // 4) % 4) * (2 * T) + ((line // 2) % 2) * T
        target = jnp.where(chosen < 0.0, -1.0, chosen + place.astype(F32))
        hot = (iota((OB, 8 * T), 1).astype(F32) == target).astype(F32).astype(BF16)
        onehot[rows, :] = hot
        send_x[rows, :] = jnp.dot(hot, xcat[...], preferred_element_type=F32).astype(BF16)

    here = pl.ds(pl.multiple_of(me * 16, 16), 16)

    def keep(src, dst, osem):
        own = pltpu.make_async_copy(src.at[here], dst.at[here], osem)
        own.start()
        return own

    def exchange(src, dst, ssem, rsem, begin_at=1, end_at=E):
        def one(k, carry):
            peer = lax.rem(me + k, E)
            pltpu.make_async_remote_copy(
                src_ref=src.at[pl.ds(pl.multiple_of(peer * 16, 16), 16)],
                dst_ref=dst.at[here],
                send_sem=ssem,
                recv_sem=rsem,
                device_id=(z, peer),
                device_id_type=MESH,
            ).start()
            return carry

        lax.fori_loop(begin_at, end_at, one, 0)

    def arrived(dst, rsem, own):
        own.wait()
        whole = dst.at[pl.ds(0, (E - 1) * 16)]
        pltpu.make_async_copy(whole, whole, rsem).wait()

    exchange(send_x, got_x, fwd_ssem.at[0], fwd_rsem.at[0])
    own_x = keep(send_x, got_x, own_sem.at[0])
    own_g = []
    pltpu.make_async_copy(gcat, gcat, in_sem.at[3]).wait()
    for half in range(2):
        for blk in range(E * 16 // OB):
            rows = pl.ds(blk * OB, OB)
            send_g[half, rows, :] = jnp.dot(
                onehot[rows, :], gcat[half], preferred_element_type=F32
            ).astype(BF16)
        src, dst = send_g.at[half], got_g.at[half]
        exchange(src, dst, fwd_ssem.at[1 + half], fwd_rsem.at[1 + half])
        own_g.append(keep(src, dst, own_sem.at[1 + half]))

    r = iota((BR, BR), 0)
    c = iota((BR, BR), 1)
    perm = (
        c == ((r // 4) % BP) * 16 + (r // BO) * 4 + r % 4
    ).astype(F32).astype(BF16)
    perm_t = (
        r == ((c // 4) % BP) * 16 + (c // BO) * 4 + c % 4
    ).astype(F32).astype(BF16)

    for copy in weights:
        copy.wait()
    arrived(got_x, fwd_rsem.at[0], own_x)
    for blk in range(NB):
        moved = jnp.dot(perm, got_x[blk * BR : (blk + 1) * BR, :], preferred_element_type=F32)
        for q in range(4):
            xs[blk * BO : (blk + 1) * BO, q * Q : (q + 1) * Q] = moved[
                q * BO : (q + 1) * BO
            ].astype(BF16)
    FT = min(256, F)
    for ft in range(F // FT):
        cols = slice(ft * FT, (ft + 1) * FT)
        h1 = jnp.dot(xs[...], wg[:, cols], preferred_element_type=F32)
        h3 = jnp.dot(xs[...], wu[:, cols], preferred_element_type=F32)
        sig = jax.nn.sigmoid(h1)
        gated = h1 * sig
        act_t[cols, :] = (gated * h3).astype(BF16).T
        coef3[:, cols] = gated
        coef1[:, cols] = h3 * sig * (1.0 + h1 * (1.0 - sig))
    for q in range(4):
        xs_t[q * Q : (q + 1) * Q, :] = xs[:, q * Q : (q + 1) * Q].T

    def take_grads(half):
        arrived(got_g.at[half], fwd_rsem.at[1 + half], own_g[half])
        for blk in range(NB):
            moved = jnp.dot(
                perm, got_g[half, blk * BR : (blk + 1) * BR, :], preferred_element_type=F32
            )
            scale = gates[blk * BO : (blk + 1) * BO, :]
            for q in range(4):
                left = half * (D // 2) + q * (Q // 2)
                dy[blk * BO : (blk + 1) * BO, left : left + Q // 2] = (
                    moved[q * BO : (q + 1) * BO] * scale
                ).astype(BF16)

    parts = (part_g, part_u, part_d0, part_d1)
    rings = (ring_g, ring_u, ring_d0, ring_d1)
    heights = (D // G, D // G, F // G, F // G)
    starts = ((0, 1, 0, 1), (1, 0, 1, 0))

    def piece(p, chunk):
        return pl.ds(pl.multiple_of(chunk * heights[p], heights[p]), heights[p])

    def forward(way, p, step, src):
        pltpu.make_async_remote_copy(
            src_ref=src,
            dst_ref=rings[p].at[way, step],
            send_sem=ring_ssem.at[way, p, step],
            recv_sem=ring_rsem.at[way, p, step],
            device_id=(z_right if way == 0 else z_left, me),
            device_id_type=MESH,
        ).start()

    def ring_copy(way, p, step):
        return pltpu.make_async_remote_copy(
            src_ref=rings[p].at[way, step],
            dst_ref=rings[p].at[way, step],
            send_sem=ring_ssem.at[way, p, step],
            recv_sem=ring_rsem.at[way, p, step],
            device_id=(z_right if way == 0 else z_left, me),
            device_id_type=MESH,
        )

    def chunk_at(way, step):
        if way == 0:
            return lax.rem(z + S - step + G, G)
        return lax.rem(z + S + step, G)

    def pass_on(way, p, step):
        ring_copy(way, p, step - 1).wait_recv()
        held = rings[p].at[way, step - 1]
        held[...] = (
            held[...].astype(F32) + parts[p][piece(p, chunk_at(way, step)), :].astype(F32)
        ).astype(BF16)
        forward(way, p, step, held)

    halves = (slice(0, D // 2), slice(D // 2, D))

    def down_part(half):
        for ft in range(F // FT):
            rows = slice(ft * FT, (ft + 1) * FT)
            parts[2 + half][rows, :] = (
                jnp.dot(act_t[rows, :], dy[:, halves[half]], preferred_element_type=F32) * factor
            ).astype(BF16)

    def enter(way, p):
        step = starts[way][p]
        forward(way, p, step, parts[p].at[piece(p, chunk_at(way, step))])

    take_grads(0)
    down_part(0)
    enter(0, 2)
    enter(1, 2)
    for ft in range(F // FT):
        cols = slice(ft * FT, (ft + 1) * FT)
        dacc[:, cols] = lax.dot_general(
            dy[:, halves[0]], wd[cols, halves[0]], contract_cols, preferred_element_type=F32
        )
    pass_on(0, 2, 1)
    if S > 2:
        pass_on(0, 2, 2)
        pass_on(1, 2, 2)

    take_grads(1)
    down_part(1)
    enter(1, 3)
    enter(0, 3)
    for ft in range(F // FT):
        cols = slice(ft * FT, (ft + 1) * FT)
        dact = dacc[:, cols] + lax.dot_general(
            dy[:, halves[1]], wd[cols, halves[1]], contract_cols, preferred_element_type=F32
        )
        dh1[:, cols] = (dact * coef1[:, cols]).astype(BF16)
        dh3[:, cols] = (dact * coef3[:, cols]).astype(BF16)
    for p, part, dh in ((0, part_g, dh1), (1, part_u, dh3)):
        for q in range(4):
            rows = slice(q * Q, (q + 1) * Q)
            part[rows, :] = (
                jnp.dot(xs_t[rows, :], dh[...], preferred_element_type=F32) * factor
            ).astype(BF16)
        enter(p, p)
        enter(1 - p, p)
    if S > 3:
        pass_on(0, 2, 3)
        pass_on(1, 2, 3)
    order = ((1, 3), (0, 0), (1, 1), (0, 3), (1, 0), (0, 1))
    for way, p in order[:3]:
        pass_on(way, p, 1)

    for q in range(4):
        rows = slice(q * Q, (q + 1) * Q)
        dx = (
            lax.dot_general(dh1[...], wg[rows, :], contract_cols, preferred_element_type=F32)
            + lax.dot_general(dh3[...], wu[rows, :], contract_cols, preferred_element_type=F32)
        ).astype(BF16)
        for blk in range(NB):
            dx_cat[blk * BR + q * BO : blk * BR + (q + 1) * BO, :] = dx[blk * BO : (blk + 1) * BO]
    for blk in range(NB):
        rows = slice(blk * BR, (blk + 1) * BR)
        send_r[rows, :] = jnp.dot(
            perm_t, dx_cat[rows, :], preferred_element_type=F32
        ).astype(BF16)
    own_r = keep(send_r, got_r, own_sem.at[3])
    lead = max(S - 4, 0)
    per = -(-(E - 1) // max(lead, 1))

    def ring_step(step, carry):
        for way, p in order[:3]:
            pass_on(way, p, step)
        begin_at = 1 + (step - 2) * per
        exchange(send_r, got_r, ret_ssem, ret_rsem, begin_at, jnp.minimum(begin_at + per, E))
        for way in range(2):
            pass_on(way, 2, step + 2)
        for way, p in order[3:]:
            pass_on(way, p, step)
        return carry

    def last_steps(step, carry):
        for way, p in order:
            pass_on(way, p, step)
        return carry

    if lead:
        lax.fori_loop(2, 2 + lead, ring_step, 0)
    else:
        exchange(send_r, got_r, ret_ssem, ret_rsem)
    lax.fori_loop(2 + lead, S, last_steps, 0)

    arrived(got_r, ret_rsem, own_r)
    summed = lax.dot_general(onehot[...], got_r[...], contract_rows, preferred_element_type=F32)
    for m in range(2):
        for q in range(4):
            tok_ref[m, :, q * Q : (q + 1) * Q] = summed[
                (q * 2 + m) * T : (q * 2 + m + 1) * T
            ].astype(BF16)

    def finish(p):
        ring_copy(0, p, S - 1).wait_recv()
        ring_copy(1, p, S - 1).wait_recv()
        return (
            rings[p][0, S - 1].astype(F32)
            + rings[p][1, S - 1].astype(F32)
            + parts[p][piece(p, z), :].astype(F32)
        ).astype(BF16)

    down_ref[0, :, 0 : D // 2] = finish(2)
    down_ref[0, :, D // 2 : D] = finish(3)
    gate_ref[0] = finish(0)
    up_ref[0] = finish(1)

    if RW > 1:
        pltpu.make_async_copy(near, near, ids_ssem.at[0]).wait()
    pltpu.make_async_copy(rest, rest, ids_ssem.at[1]).wait()
    sent = [(send_g.at[half], fwd_ssem.at[1 + half]) for half in range(2)]
    for src, sem in [(send_x, fwd_ssem.at[0]), (send_r, ret_ssem)] + sent:
        whole = src.at[pl.ds(0, (E - 1) * 16)]
        pltpu.make_async_copy(whole, whole, sem).wait()
    for way in range(2):
        for p in range(4):
            for step in range(starts[way][p], S):
                ring_copy(way, p, step).wait_send()


def body(activations, out_grads, chosen_ids, gate_logits, w_gate, w_up, w_down):
    E = lax.axis_size("expert")
    G = lax.axis_size("dp")
    T, D = activations.shape[1:]
    F = w_gate.shape[-1]
    C = chosen_ids.shape[-1]
    Q, S, R4, R16 = D // 4, G // 2, 4 * E, 16 * E
    vmem = pl.BlockSpec(memory_space=pltpu.VMEM)
    hbm = pl.BlockSpec(memory_space=pltpu.HBM)
    V = pltpu.VMEM
    dma = pltpu.SemaphoreType.DMA
    scratch = [
        V((2, 1, 1, C), jnp.int32), V((2, 1, 1, C), jnp.int32),
        V((2, 128), jnp.int32), V((2, 128), jnp.int32),
        V((E, 2, 128), jnp.int32), V((2, E, 128), jnp.int32),
        V((D, F), BF16), V((D, F), BF16), V((F, D), BF16),
        V((8 * T, Q), BF16), V((2, 8 * T, Q // 2), BF16), V((R16, 8 * T), BF16),
        V((R16, Q), BF16), V((2, R16, Q // 2), BF16),
        V((R16, Q), BF16), V((2, R16, Q // 2), BF16), V((R4, F), F32),
        V((R4, D), BF16), V((D, R4), BF16), V((R4, D), BF16), V((F, R4), BF16),
        V((R4, F), F32), V((R4, F), F32), V((R4, F), BF16), V((R4, F), BF16), V((R4, 1), F32),
        V((R16, Q), BF16), V((R16, Q), BF16), V((R16, Q), BF16),
        V((D, F), BF16), V((D, F), BF16), V((F, D // 2), BF16), V((F, D // 2), BF16),
        V((2, S, D // G, F), BF16), V((2, S, D // G, F), BF16),
        V((2, S, F // G, D // 2), BF16), V((2, S, F // G, D // 2), BF16),
        dma((3,)), dma((4,)), dma((2,)), dma((2,)), dma((3,)), dma((3,)), dma((4,)), dma, dma,
        dma((2, 4, S)), dma((2, 4, S)),
    ]
    shape = jax.ShapeDtypeStruct
    return pl.pallas_call(
        functools.partial(fused, (E, G, T, D, F, C)),
        out_shape=(
            shape((2, T, D), BF16),
            shape((1, D // G, F), BF16),
            shape((1, D // G, F), BF16),
            shape((1, F // G, D), BF16),
        ),
        in_specs=[hbm] * 7,
        out_specs=(vmem, vmem, vmem, vmem),
        scratch_shapes=scratch,
        compiler_params=pltpu.CompilerParams(
            collective_id=0, has_side_effects=True, vmem_limit_bytes=64 * 1024 * 1024
        ),
    )(chosen_ids, gate_logits, activations, out_grads, w_gate, w_up, w_down)


def solution(mesh):
    placed = (
        P(None, ("dp", "expert"), None),
        P(None, ("dp", "expert"), None),
        P(None, "dp", "expert", None),
        P(None, "dp", "expert", None),
        P("expert", None, None),
        P("expert", None, None),
        P("expert", None, None),
    )
    return jax.shard_map(
        body,
        mesh=mesh,
        in_specs=placed,
        out_specs=(
            P(None, ("dp", "expert"), None),
            P("expert", "dp", None),
            P("expert", "dp", None),
            P("expert", "dp", None),
        ),
        check_vma=False,
    )
```

```python
import functools
import math

import jax
import jax.numpy as jnp
from jax import lax
from jax.experimental import pallas as pl
from jax.experimental.pallas import tpu as pltpu
from jax.sharding import PartitionSpec as P

MESH = pl.DeviceIdType.MESH
BF16 = jnp.bfloat16
F32 = jnp.float32
contract_rows = (((0,), (0,)), ((), ()))
contract_cols = (((1,), (1,)), ((), ()))


def iota(shape, axis):
    return lax.broadcasted_iota(jnp.int32, shape, axis)


def fused(
    sizes,
    ids_hbm, logits_hbm, x_hbm, g_hbm, wg_hbm, wu_hbm, wd_hbm,
    tok_ref, gate_ref, up_ref, down_ref,
    ids_ref, logits_ref, ids_send, logits_pad, ids_all, ids_flat,
    wg, wu, wd,
    xcat, gcat, onehot, send_x, send_g, got_x, got_g,
    xs, xs_t, dy, act_t, coef1, coef3, dh1, dh3, gates,
    dx_cat, send_r, got_r,
    part_g, part_u, part_d0, part_d1,
    ring_g, ring_u, ring_d0, ring_d1,
    w_sem, in_sem, ids_ssem, ids_rsem, fwd_ssem, fwd_rsem, own_sem, ret_ssem, ret_rsem,
    ring_ssem, ring_rsem,
):
    E, G, T, D, F, C = sizes
    Q = D // 4
    S = G // 2
    R4 = 4 * E
    BP = min(16, E)
    BR = BP * 16
    BO = BP * 4
    NB = E // BP
    factor = 1.0 / math.sqrt(G * 2 * C)
    me = lax.axis_index("expert")
    z = lax.axis_index("dp")
    z_right = lax.rem(z + 1, G)
    z_left = lax.rem(z + G - 1, G)

    RW = min(8, E // 2)
    CW = E // RW
    row_at = me // RW
    col_at = lax.rem(me, RW)

    small = [
        pltpu.make_async_copy(src, dst, in_sem.at[k])
        for k, (src, dst) in enumerate(((ids_hbm, ids_ref), (logits_hbm, logits_ref)))
    ]
    for copy in small:
        copy.start()

    def row_mate(k):
        return row_at * RW + lax.rem(col_at + k, RW)

    def col_mate(k):
        return lax.rem(row_at + k, CW) * RW + col_at

    barrier = pltpu.get_barrier_semaphore()
    mates = [(z, row_mate(k)) for k in range(1, RW)] + [(z, col_mate(k)) for k in range(1, CW)]
    for other in mates + [(z_right, me), (z_left, me)]:
        pl.semaphore_signal(barrier, inc=1, device_id=other, device_id_type=MESH)

    for m in range(2):
        for q in range(4):
            rows = pl.ds((q * 2 + m) * T, T)
            pltpu.make_async_copy(
                x_hbm.at[m, :, pl.ds(q * Q, Q)], xcat.at[rows, :], in_sem.at[2]
            ).start()
    for copy in small:
        copy.wait()

    ids_send[...] = jnp.full(ids_send.shape, -1, jnp.int32)
    logits_pad[...] = jnp.zeros(logits_pad.shape, jnp.int32)
    for m in range(2):
        ids_send[m : m + 1, 0:C] = ids_ref[m, 0]
        logits_pad[m : m + 1, 0:C] = logits_ref[m, 0]
    ids_all[pl.ds(me, 1)] = ids_send[...][None]

    pl.semaphore_wait(barrier, RW - 1 + CW - 1 + 2)

    for k in range(1, RW):
        pltpu.make_async_remote_copy(
            src_ref=ids_send,
            dst_ref=ids_all.at[me],
            send_sem=ids_ssem.at[0],
            recv_sem=ids_rsem.at[0],
            device_id=(z, row_mate(k)),
            device_id_type=MESH,
        ).start()
    near = ids_all.at[pl.ds(0, max(RW - 1, 1))]
    if RW > 1:
        pltpu.make_async_copy(near, near, ids_rsem.at[0]).wait()
    ours = ids_all.at[pl.ds(row_at * RW, RW)]
    for k in range(1, CW):
        pltpu.make_async_remote_copy(
            src_ref=ours,
            dst_ref=ours,
            send_sem=ids_ssem.at[1],
            recv_sem=ids_rsem.at[1],
            device_id=(z, col_mate(k)),
            device_id_type=MESH,
        ).start()

    for m in range(2):
        for q in range(4):
            rows = pl.ds((q * 2 + m) * T, T)
            pltpu.make_async_copy(
                g_hbm.at[m, :, pl.ds(q * Q, Q)], gcat.at[rows, :], in_sem.at[3]
            ).start()
    weights = [
        pltpu.make_async_copy(src.at[0], dst, w_sem.at[k])
        for k, (src, dst) in enumerate(((wg_hbm, wg), (wu_hbm, wu), (wd_hbm, wd)))
    ]
    for copy in weights:
        copy.start()
    row = iota((R4, 128), 0)
    micro_row = (row // 2) % 2
    mine = jnp.where(micro_row == 0, ids_send[0:1, :], ids_send[1:2, :]).astype(F32)
    marks = jnp.where(micro_row == 0, logits_pad[0:1, :], logits_pad[1:2, :]).astype(F32)
    low = ((row // 4) * T).astype(F32)
    inside = (mine >= low) & (mine < low + float(T))
    first = jnp.min(jnp.where(inside, mine, 1e6), axis=1, keepdims=True)
    last = jnp.max(jnp.where(inside, mine, -1.0), axis=1, keepdims=True)
    pick = jnp.where(row % 2 == 0, first, last)
    logit = jnp.sum(jnp.where(inside & (mine == pick), marks, 0.0), axis=1, keepdims=True)
    gates[...] = jax.nn.sigmoid(logit * (1.0 / 4096.0))

    rest = ids_all.at[pl.ds(0, (CW - 1) * RW)]
    pltpu.make_async_copy(rest, rest, ids_rsem.at[1]).wait()

    for e in range(E):
        for m in range(2):
            ids_flat[m, e : e + 1, :] = ids_all[e, m : m + 1, :]
    lane = iota((E, 128), 1)
    table = jnp.full((E, 128), -1.0, F32)
    base = (me * T).astype(F32)
    for m in range(2):
        local = ids_flat[m].astype(F32) - base
        inside = (local >= 0.0) & (local < float(T))
        first = jnp.min(jnp.where(inside, local, 1e6), axis=1, keepdims=True)
        last = jnp.max(jnp.where(inside, local, -1.0), axis=1, keepdims=True)
        first_ok = jnp.where(first < 1e5, first, -1.0)
        last_ok = jnp.where(last > first, last, -1.0)
        table = jnp.where(lane == 2 * m, first_ok, table)
        table = jnp.where(lane == 2 * m + 1, last_ok, table)
    table = table.astype(BF16)

    here = pl.ds(pl.multiple_of(me * 16, 16), 16)

    def keep(src, dst, osem):
        own = pltpu.make_async_copy(src.at[here], dst.at[here], osem)
        own.start()
        return own

    def exchange(src, dst, ssem, rsem):
        def one(k, carry):
            peer = lax.rem(me + k, E)
            pltpu.make_async_remote_copy(
                src_ref=src.at[pl.ds(pl.multiple_of(peer * 16, 16), 16)],
                dst_ref=dst.at[here],
                send_sem=ssem,
                recv_sem=rsem,
                device_id=(z, peer),
                device_id_type=MESH,
            ).start()
            return carry

        lax.fori_loop(1, E, one, 0)

    def arrived(dst, rsem, own):
        own.wait()
        whole = dst.at[pl.ds(0, (E - 1) * 16)]
        pltpu.make_async_copy(whole, whole, rsem).wait()

    OB = RW * 16
    line = iota((OB, 1), 0)
    place = (((line // 4) % 4) * (2 * T) + ((line // 2) % 2) * T).astype(F32)
    mine_lane = iota((OB, 128), 1) == iota((OB, 128), 0) % 4
    offsets = [sign * step for step in range(1, CW) for sign in (1, -1)][: CW - 1] + [0]

    def send_row(row, src, dst, ssem, rsem, begin_at):
        def one(k, carry):
            peer = row * RW + lax.rem(col_at + k, RW)
            pltpu.make_async_remote_copy(
                src_ref=src.at[pl.ds(pl.multiple_of(peer * 16, 16), 16)],
                dst_ref=dst.at[here],
                send_sem=ssem,
                recv_sem=rsem,
                device_id=(z, peer),
                device_id_type=MESH,
            ).start()
            return carry

        lax.fori_loop(begin_at, RW, one, 0)

    pltpu.make_async_copy(xcat, xcat, in_sem.at[2]).wait()
    for offset in offsets:
        row = lax.rem(row_at + offset + CW, CW)
        rows = pl.ds(pl.multiple_of(row * OB, OB), OB)
        spread = (line // 16 + row * RW == iota((OB, E), 1)).astype(F32).astype(BF16)
        values = jnp.dot(spread, table, preferred_element_type=F32)
        chosen = jnp.sum(jnp.where(mine_lane, values, 0.0), axis=1, keepdims=True)
        target = jnp.where(chosen < 0.0, -1.0, chosen + place)
        hot = (iota((OB, 8 * T), 1).astype(F32) == target).astype(F32).astype(BF16)
        onehot[rows, :] = hot
        send_x[rows, :] = jnp.dot(hot, xcat[...], preferred_element_type=F32).astype(BF16)
        send_row(row, send_x, got_x, fwd_ssem.at[0], fwd_rsem.at[0], 0 if offset else 1)
    own_x = keep(send_x, got_x, own_sem.at[0])
    pltpu.make_async_copy(gcat, gcat, in_sem.at[3]).wait()
    for offset in offsets:
        row = lax.rem(row_at + offset + CW, CW)
        rows = pl.ds(pl.multiple_of(row * OB, OB), OB)
        send_g[rows, :] = jnp.dot(
            onehot[rows, :], gcat[...], preferred_element_type=F32
        ).astype(BF16)
        send_row(row, send_g, got_g, fwd_ssem.at[1], fwd_rsem.at[1], 0 if offset else 1)
    own_g = keep(send_g, got_g, own_sem.at[1])

    r = iota((BR, BR), 0)
    c = iota((BR, BR), 1)
    perm = (
        c == ((r // 4) % BP) * 16 + (r // BO) * 4 + r % 4
    ).astype(F32).astype(BF16)
    perm_t = (
        r == ((c // 4) % BP) * 16 + (c // BO) * 4 + c % 4
    ).astype(F32).astype(BF16)

    for copy in weights:
        copy.wait()
    arrived(got_x, fwd_rsem.at[0], own_x)
    for blk in range(NB):
        moved = jnp.dot(perm, got_x[blk * BR : (blk + 1) * BR, :], preferred_element_type=F32)
        for q in range(4):
            xs[blk * BO : (blk + 1) * BO, q * Q : (q + 1) * Q] = moved[
                q * BO : (q + 1) * BO
            ].astype(BF16)
    FT = min(256, F)
    for ft in range(F // FT):
        cols = slice(ft * FT, (ft + 1) * FT)
        h1 = jnp.dot(xs[...], wg[:, cols], preferred_element_type=F32)
        h3 = jnp.dot(xs[...], wu[:, cols], preferred_element_type=F32)
        sig = jax.nn.sigmoid(h1)
        gated = h1 * sig
        act_t[cols, :] = (gated * h3).astype(BF16).T
        coef3[:, cols] = gated
        coef1[:, cols] = h3 * sig * (1.0 + h1 * (1.0 - sig))
    for q in range(4):
        xs_t[q * Q : (q + 1) * Q, :] = xs[:, q * Q : (q + 1) * Q].T

    arrived(got_g, fwd_rsem.at[1], own_g)
    for blk in range(NB):
        moved = jnp.dot(perm, got_g[blk * BR : (blk + 1) * BR, :], preferred_element_type=F32)
        scale = gates[blk * BO : (blk + 1) * BO, :]
        for q in range(4):
            dy[blk * BO : (blk + 1) * BO, q * Q : (q + 1) * Q] = (
                moved[q * BO : (q + 1) * BO] * scale
            ).astype(BF16)

    parts = (part_g, part_u, part_d0, part_d1)
    rings = (ring_g, ring_u, ring_d0, ring_d1)
    heights = (D // G, D // G, F // G, F // G)
    starts = ((0, 1, 0, 1), (1, 0, 1, 0))

    def piece(p, chunk):
        return pl.ds(pl.multiple_of(chunk * heights[p], heights[p]), heights[p])

    def forward(way, p, step, src):
        pltpu.make_async_remote_copy(
            src_ref=src,
            dst_ref=rings[p].at[way, step],
            send_sem=ring_ssem.at[way, p, step],
            recv_sem=ring_rsem.at[way, p, step],
            device_id=(z_right if way == 0 else z_left, me),
            device_id_type=MESH,
        ).start()

    def ring_copy(way, p, step):
        return pltpu.make_async_remote_copy(
            src_ref=rings[p].at[way, step],
            dst_ref=rings[p].at[way, step],
            send_sem=ring_ssem.at[way, p, step],
            recv_sem=ring_rsem.at[way, p, step],
            device_id=(z_right if way == 0 else z_left, me),
            device_id_type=MESH,
        )

    far = lax.rem(z + S, G)

    def begin(p):
        forward(starts[0][p], p, 0, parts[p].at[piece(p, far)])

    for ft in range(F // FT):
        rows = slice(ft * FT, (ft + 1) * FT)
        for half, part in ((0, part_d0), (1, part_d1)):
            part[rows, :] = (
                jnp.dot(
                    act_t[rows, :],
                    dy[:, half * (D // 2) : (half + 1) * (D // 2)],
                    preferred_element_type=F32,
                )
                * factor
            ).astype(BF16)
    begin(2)
    begin(3)
    for ft in range(F // FT):
        cols = slice(ft * FT, (ft + 1) * FT)
        dact = lax.dot_general(dy[...], wd[cols, :], contract_cols, preferred_element_type=F32)
        dh1[:, cols] = (dact * coef1[:, cols]).astype(BF16)
        dh3[:, cols] = (dact * coef3[:, cols]).astype(BF16)
    for p, part, dh in ((0, part_g, dh1), (1, part_u, dh3)):
        for q in range(4):
            rows = slice(q * Q, (q + 1) * Q)
            part[rows, :] = (
                jnp.dot(xs_t[rows, :], dh[...], preferred_element_type=F32) * factor
            ).astype(BF16)
        begin(p)

    def chunk_at(way, step):
        if way == 0:
            return lax.rem(z + S - step + G, G)
        return lax.rem(z + S + step, G)

    def pass_on(way, p, step):
        ring_copy(way, p, step - 1).wait_recv()
        held = rings[p].at[way, step - 1]
        held[...] = (
            held[...].astype(F32) + parts[p][piece(p, chunk_at(way, step)), :].astype(F32)
        ).astype(BF16)
        forward(way, p, step, held)

    order = ((0, 2), (1, 3), (0, 0), (1, 1), (0, 3), (1, 2), (0, 1), (1, 0))
    for way, p in order:
        if starts[way][p] == 1:
            forward(way, p, 1, parts[p].at[piece(p, chunk_at(way, 1))])
    for way, p in order:
        if starts[way][p] == 0:
            pass_on(way, p, 1)

    for q in range(4):
        rows = slice(q * Q, (q + 1) * Q)
        dx = (
            lax.dot_general(dh1[...], wg[rows, :], contract_cols, preferred_element_type=F32)
            + lax.dot_general(dh3[...], wu[rows, :], contract_cols, preferred_element_type=F32)
        ).astype(BF16)
        for blk in range(NB):
            dx_cat[blk * BR + q * BO : blk * BR + (q + 1) * BO, :] = dx[blk * BO : (blk + 1) * BO]
    for blk in range(NB):
        rows = slice(blk * BR, (blk + 1) * BR)
        send_r[rows, :] = jnp.dot(
            perm_t, dx_cat[rows, :], preferred_element_type=F32
        ).astype(BF16)
    exchange(send_r, got_r, ret_ssem, ret_rsem)
    own_r = keep(send_r, got_r, own_sem.at[2])

    def ring_step(step, carry):
        for way, p in order:
            pass_on(way, p, step)
        return carry

    lax.fori_loop(2, S, ring_step, 0)

    arrived(got_r, ret_rsem, own_r)
    summed = lax.dot_general(onehot[...], got_r[...], contract_rows, preferred_element_type=F32)
    for m in range(2):
        for q in range(4):
            tok_ref[m, :, q * Q : (q + 1) * Q] = summed[
                (q * 2 + m) * T : (q * 2 + m + 1) * T
            ].astype(BF16)

    def finish(p):
        ring_copy(0, p, S - 1).wait_recv()
        ring_copy(1, p, S - 1).wait_recv()
        return (
            rings[p][0, S - 1].astype(F32)
            + rings[p][1, S - 1].astype(F32)
            + parts[p][piece(p, z), :].astype(F32)
        ).astype(BF16)

    down_ref[0, :, 0 : D // 2] = finish(2)
    down_ref[0, :, D // 2 : D] = finish(3)
    gate_ref[0] = finish(0)
    up_ref[0] = finish(1)

    if RW > 1:
        pltpu.make_async_copy(near, near, ids_ssem.at[0]).wait()
    pltpu.make_async_copy(rest, rest, ids_ssem.at[1]).wait()
    for src, sem in ((send_x, fwd_ssem.at[0]), (send_g, fwd_ssem.at[1]), (send_r, ret_ssem)):
        whole = src.at[pl.ds(0, (E - 1) * 16)]
        pltpu.make_async_copy(whole, whole, sem).wait()
    for way in range(2):
        for p in range(4):
            for step in range(starts[way][p], S):
                ring_copy(way, p, step).wait_send()


def settle(*refs):
    number = len(refs) // 2
    sems = refs[-1]
    copies = [
        pltpu.make_async_copy(refs[k], refs[number + k], sems.at[k]) for k in range(number)
    ]
    for copy in copies:
        copy.start()
    for copy in copies:
        copy.wait()


def body(activations, out_grads, chosen_ids, gate_logits, w_gate, w_up, w_down):
    E = lax.axis_size("expert")
    G = lax.axis_size("dp")
    T, D = activations.shape[1:]
    F = w_gate.shape[-1]
    C = chosen_ids.shape[-1]
    Q, S, R4, R16 = D // 4, G // 2, 4 * E, 16 * E
    vmem = pl.BlockSpec(memory_space=pltpu.VMEM)
    hbm = pl.BlockSpec(memory_space=pltpu.HBM)
    V = pltpu.VMEM
    dma = pltpu.SemaphoreType.DMA
    scratch = [
        V((2, 1, 1, C), jnp.int32), V((2, 1, 1, C), jnp.int32),
        V((2, 128), jnp.int32), V((2, 128), jnp.int32),
        V((E, 2, 128), jnp.int32), V((2, E, 128), jnp.int32),
        V((D, F), BF16), V((D, F), BF16), V((F, D), BF16),
        V((8 * T, Q), BF16), V((8 * T, Q), BF16), V((R16, 8 * T), BF16),
        V((R16, Q), BF16), V((R16, Q), BF16), V((R16, Q), BF16), V((R16, Q), BF16),
        V((R4, D), BF16), V((D, R4), BF16), V((R4, D), BF16), V((F, R4), BF16),
        V((R4, F), F32), V((R4, F), F32), V((R4, F), BF16), V((R4, F), BF16), V((R4, 1), F32),
        V((R16, Q), BF16), V((R16, Q), BF16), V((R16, Q), BF16),
        V((D, F), BF16), V((D, F), BF16), V((F, D // 2), BF16), V((F, D // 2), BF16),
        V((2, S, D // G, F), BF16), V((2, S, D // G, F), BF16),
        V((2, S, F // G, D // 2), BF16), V((2, S, F // G, D // 2), BF16),
        dma((3,)), dma((4,)), dma((2,)), dma((2,)), dma((2,)), dma((2,)), dma((3,)), dma, dma,
        dma((2, 4, S)), dma((2, 4, S)),
    ]
    shape = jax.ShapeDtypeStruct
    results = pl.pallas_call(
        functools.partial(fused, (E, G, T, D, F, C)),
        out_shape=(
            shape((2, T, D), BF16),
            shape((1, D // G, F), BF16),
            shape((1, D // G, F), BF16),
            shape((1, F // G, D), BF16),
        ),
        in_specs=[hbm] * 7,
        out_specs=(vmem, vmem, vmem, vmem),
        scratch_shapes=scratch,
        compiler_params=pltpu.CompilerParams(
            collective_id=0, has_side_effects=True, vmem_limit_bytes=64 * 1024 * 1024
        ),
    )(chosen_ids, gate_logits, activations, out_grads, w_gate, w_up, w_down)
    return pl.pallas_call(
        settle,
        out_shape=tuple(shape(item.shape, item.dtype) for item in results),
        in_specs=[hbm] * 4,
        out_specs=(hbm,) * 4,
        scratch_shapes=[dma((4,))],
        compiler_params=pltpu.CompilerParams(vmem_limit_bytes=64 * 1024 * 1024),
    )(*results)


def solution(mesh):
    placed = (
        P(None, ("dp", "expert"), None),
        P(None, ("dp", "expert"), None),
        P(None, "dp", "expert", None),
        P(None, "dp", "expert", None),
        P("expert", None, None),
        P("expert", None, None),
        P("expert", None, None),
    )
    return jax.shard_map(
        body,
        mesh=mesh,
        in_specs=placed,
        out_specs=(
            P(None, ("dp", "expert"), None),
            P("expert", "dp", None),
            P("expert", "dp", None),
            P("expert", "dp", None),
        ),
        check_vma=False,
    )
```

```python
import functools
import math

import jax
import jax.numpy as jnp
from jax import lax
from jax.experimental import pallas as pl
from jax.experimental.pallas import tpu as pltpu
from jax.sharding import PartitionSpec as P

MESH = pl.DeviceIdType.MESH
BF16 = jnp.bfloat16
F32 = jnp.float32
contract_rows = (((0,), (0,)), ((), ()))
contract_cols = (((1,), (1,)), ((), ()))


def iota(shape, axis):
    return lax.broadcasted_iota(jnp.int32, shape, axis)


def fused(
    sizes,
    ids_hbm, logits_hbm, x_hbm, g_hbm, wg_hbm, wu_hbm, wd_hbm,
    tok_ref, gate_ref, up_ref, down_ref,
    ids_ref, logits_ref, ids_send, logits_pad, ids_all, ids_flat,
    wg, wu, wd,
    xcat, gcat, onehot, send_x, send_g, got_x, got_g,
    xs, xs_t, dy, act_t, coef1, coef3, dh1, dh3, gates,
    dx_cat, send_r, got_r,
    part_g, part_u, part_d0, part_d1,
    ring_g, ring_u, ring_d0, ring_d1,
    w_sem, in_sem, ids_ssem, ids_rsem, fwd_ssem, fwd_rsem, own_sem, ret_ssem, ret_rsem,
    ring_ssem, ring_rsem,
):
    E, G, T, D, F, C = sizes
    Q = D // 4
    S = G // 2
    R4 = 4 * E
    BP = min(16, E)
    BR = BP * 16
    BO = BP * 4
    NB = E // BP
    factor = 1.0 / math.sqrt(G * 2 * C)
    me = lax.axis_index("expert")
    z = lax.axis_index("dp")
    z_right = lax.rem(z + 1, G)
    z_left = lax.rem(z + G - 1, G)

    RW = min(8, E // 2)
    CW = E // RW
    row_at = me // RW
    col_at = lax.rem(me, RW)

    small = [
        pltpu.make_async_copy(src, dst, in_sem.at[k])
        for k, (src, dst) in enumerate(((ids_hbm, ids_ref), (logits_hbm, logits_ref)))
    ]
    for copy in small:
        copy.start()

    def row_mate(k):
        return row_at * RW + lax.rem(col_at + k, RW)

    def col_mate(k):
        return lax.rem(row_at + k, CW) * RW + col_at

    barrier = pltpu.get_barrier_semaphore()
    mates = [(z, row_mate(k)) for k in range(1, RW)] + [(z, col_mate(k)) for k in range(1, CW)]
    for other in mates + [(z_right, me), (z_left, me)]:
        pl.semaphore_signal(barrier, inc=1, device_id=other, device_id_type=MESH)

    for m in range(2):
        for q in range(4):
            rows = pl.ds((q * 2 + m) * T, T)
            pltpu.make_async_copy(
                x_hbm.at[m, :, pl.ds(q * Q, Q)], xcat.at[rows, :], in_sem.at[2]
            ).start()
    for copy in small:
        copy.wait()

    ids_send[...] = jnp.full(ids_send.shape, -1, jnp.int32)
    logits_pad[...] = jnp.zeros(logits_pad.shape, jnp.int32)
    for m in range(2):
        ids_send[m : m + 1, 0:C] = ids_ref[m, 0]
        logits_pad[m : m + 1, 0:C] = logits_ref[m, 0]
    ids_all[pl.ds(me, 1)] = ids_send[...][None]

    pl.semaphore_wait(barrier, RW - 1 + CW - 1 + 2)

    for k in range(1, RW):
        pltpu.make_async_remote_copy(
            src_ref=ids_send,
            dst_ref=ids_all.at[me],
            send_sem=ids_ssem.at[0],
            recv_sem=ids_rsem.at[0],
            device_id=(z, row_mate(k)),
            device_id_type=MESH,
        ).start()
    near = ids_all.at[pl.ds(0, max(RW - 1, 1))]
    if RW > 1:
        pltpu.make_async_copy(near, near, ids_rsem.at[0]).wait()
    ours = ids_all.at[pl.ds(row_at * RW, RW)]
    for k in range(1, CW):
        pltpu.make_async_remote_copy(
            src_ref=ours,
            dst_ref=ours,
            send_sem=ids_ssem.at[1],
            recv_sem=ids_rsem.at[1],
            device_id=(z, col_mate(k)),
            device_id_type=MESH,
        ).start()

    for m in range(2):
        for q in range(4):
            rows = pl.ds((q * 2 + m) * T, T)
            pltpu.make_async_copy(
                g_hbm.at[m, :, pl.ds(q * Q, Q)], gcat.at[rows, :], in_sem.at[3]
            ).start()
    row = iota((R4, 128), 0)
    micro_row = (row // 2) % 2
    mine = jnp.where(micro_row == 0, ids_send[0:1, :], ids_send[1:2, :]).astype(F32)
    marks = jnp.where(micro_row == 0, logits_pad[0:1, :], logits_pad[1:2, :]).astype(F32)
    low = ((row // 4) * T).astype(F32)
    inside = (mine >= low) & (mine < low + float(T))
    first = jnp.min(jnp.where(inside, mine, 1e6), axis=1, keepdims=True)
    last = jnp.max(jnp.where(inside, mine, -1.0), axis=1, keepdims=True)
    pick = jnp.where(row % 2 == 0, first, last)
    logit = jnp.sum(jnp.where(inside & (mine == pick), marks, 0.0), axis=1, keepdims=True)
    gates[...] = jax.nn.sigmoid(logit * (1.0 / 4096.0))

    rest = ids_all.at[pl.ds(0, (CW - 1) * RW)]
    pltpu.make_async_copy(rest, rest, ids_rsem.at[1]).wait()

    for e in range(E):
        for m in range(2):
            ids_flat[m, e : e + 1, :] = ids_all[e, m : m + 1, :]
    lane = iota((E, 128), 1)
    table = jnp.full((E, 128), -1.0, F32)
    base = (me * T).astype(F32)
    for m in range(2):
        local = ids_flat[m].astype(F32) - base
        inside = (local >= 0.0) & (local < float(T))
        first = jnp.min(jnp.where(inside, local, 1e6), axis=1, keepdims=True)
        last = jnp.max(jnp.where(inside, local, -1.0), axis=1, keepdims=True)
        first_ok = jnp.where(first < 1e5, first, -1.0)
        last_ok = jnp.where(last > first, last, -1.0)
        table = jnp.where(lane == 2 * m, first_ok, table)
        table = jnp.where(lane == 2 * m + 1, last_ok, table)
    table = table.astype(BF16)

    here = pl.ds(pl.multiple_of(me * 16, 16), 16)

    def keep(src, dst, osem):
        own = pltpu.make_async_copy(src.at[here], dst.at[here], osem)
        own.start()
        return own

    def exchange(src, dst, ssem, rsem):
        def one(k, carry):
            peer = lax.rem(me + k, E)
            pltpu.make_async_remote_copy(
                src_ref=src.at[pl.ds(pl.multiple_of(peer * 16, 16), 16)],
                dst_ref=dst.at[here],
                send_sem=ssem,
                recv_sem=rsem,
                device_id=(z, peer),
                device_id_type=MESH,
            ).start()
            return carry

        lax.fori_loop(1, E, one, 0)

    def arrived(dst, rsem, own):
        own.wait()
        whole = dst.at[pl.ds(0, (E - 1) * 16)]
        pltpu.make_async_copy(whole, whole, rsem).wait()

    OB = RW * 16
    line = iota((OB, 1), 0)
    place = (((line // 4) % 4) * (2 * T) + ((line // 2) % 2) * T).astype(F32)
    mine_lane = iota((OB, 128), 1) == iota((OB, 128), 0) % 4
    offsets = [sign * step for step in range(1, CW) for sign in (1, -1)][: CW - 1] + [0]

    def send_row(row, src, dst, ssem, rsem, begin_at):
        def one(k, carry):
            peer = row * RW + lax.rem(col_at + k, RW)
            pltpu.make_async_remote_copy(
                src_ref=src.at[pl.ds(pl.multiple_of(peer * 16, 16), 16)],
                dst_ref=dst.at[here],
                send_sem=ssem,
                recv_sem=rsem,
                device_id=(z, peer),
                device_id_type=MESH,
            ).start()
            return carry

        lax.fori_loop(begin_at, RW, one, 0)

    pltpu.make_async_copy(xcat, xcat, in_sem.at[2]).wait()
    for offset in offsets:
        row = lax.rem(row_at + offset + CW, CW)
        rows = pl.ds(pl.multiple_of(row * OB, OB), OB)
        spread = (line // 16 + row * RW == iota((OB, E), 1)).astype(F32).astype(BF16)
        values = jnp.dot(spread, table, preferred_element_type=F32)
        chosen = jnp.sum(jnp.where(mine_lane, values, 0.0), axis=1, keepdims=True)
        target = jnp.where(chosen < 0.0, -1.0, chosen + place)
        hot = (iota((OB, 8 * T), 1).astype(F32) == target).astype(F32).astype(BF16)
        onehot[rows, :] = hot
        send_x[rows, :] = jnp.dot(hot, xcat[...], preferred_element_type=F32).astype(BF16)
        send_row(row, send_x, got_x, fwd_ssem.at[0], fwd_rsem.at[0], 0 if offset else 1)
    own_x = keep(send_x, got_x, own_sem.at[0])
    weights = [
        pltpu.make_async_copy(src.at[0], dst, w_sem.at[k])
        for k, (src, dst) in enumerate(((wg_hbm, wg), (wu_hbm, wu), (wd_hbm, wd)))
    ]
    for copy in weights:
        copy.start()
    pltpu.make_async_copy(gcat, gcat, in_sem.at[3]).wait()
    for offset in offsets:
        row = lax.rem(row_at + offset + CW, CW)
        rows = pl.ds(pl.multiple_of(row * OB, OB), OB)
        send_g[rows, :] = jnp.dot(
            onehot[rows, :], gcat[...], preferred_element_type=F32
        ).astype(BF16)
        send_row(row, send_g, got_g, fwd_ssem.at[1], fwd_rsem.at[1], 0 if offset else 1)
    own_g = keep(send_g, got_g, own_sem.at[1])

    r = iota((BR, BR), 0)
    c = iota((BR, BR), 1)
    perm = (
        c == ((r // 4) % BP) * 16 + (r // BO) * 4 + r % 4
    ).astype(F32).astype(BF16)
    perm_t = (
        r == ((c // 4) % BP) * 16 + (c // BO) * 4 + c % 4
    ).astype(F32).astype(BF16)

    for copy in weights:
        copy.wait()
    arrived(got_x, fwd_rsem.at[0], own_x)
    for blk in range(NB):
        moved = jnp.dot(perm, got_x[blk * BR : (blk + 1) * BR, :], preferred_element_type=F32)
        for q in range(4):
            xs[blk * BO : (blk + 1) * BO, q * Q : (q + 1) * Q] = moved[
                q * BO : (q + 1) * BO
            ].astype(BF16)
    FT = min(256, F)
    for ft in range(F // FT):
        cols = slice(ft * FT, (ft + 1) * FT)
        h1 = jnp.dot(xs[...], wg[:, cols], preferred_element_type=F32)
        h3 = jnp.dot(xs[...], wu[:, cols], preferred_element_type=F32)
        sig = jax.nn.sigmoid(h1)
        gated = h1 * sig
        act_t[cols, :] = (gated * h3).astype(BF16).T
        coef3[:, cols] = gated
        coef1[:, cols] = h3 * sig * (1.0 + h1 * (1.0 - sig))
    for q in range(4):
        xs_t[q * Q : (q + 1) * Q, :] = xs[:, q * Q : (q + 1) * Q].T

    arrived(got_g, fwd_rsem.at[1], own_g)
    for blk in range(NB):
        moved = jnp.dot(perm, got_g[blk * BR : (blk + 1) * BR, :], preferred_element_type=F32)
        scale = gates[blk * BO : (blk + 1) * BO, :]
        for q in range(4):
            dy[blk * BO : (blk + 1) * BO, q * Q : (q + 1) * Q] = (
                moved[q * BO : (q + 1) * BO] * scale
            ).astype(BF16)

    parts = (part_g, part_u, part_d0, part_d1)
    rings = (ring_g, ring_u, ring_d0, ring_d1)
    heights = (D // G, D // G, F // G, F // G)
    starts = ((0, 1, 0, 1), (1, 0, 1, 0))

    def piece(p, chunk):
        return pl.ds(pl.multiple_of(chunk * heights[p], heights[p]), heights[p])

    def forward(way, p, step, src):
        pltpu.make_async_remote_copy(
            src_ref=src,
            dst_ref=rings[p].at[way, step],
            send_sem=ring_ssem.at[way, p, step],
            recv_sem=ring_rsem.at[way, p, step],
            device_id=(z_right if way == 0 else z_left, me),
            device_id_type=MESH,
        ).start()

    def ring_copy(way, p, step):
        return pltpu.make_async_remote_copy(
            src_ref=rings[p].at[way, step],
            dst_ref=rings[p].at[way, step],
            send_sem=ring_ssem.at[way, p, step],
            recv_sem=ring_rsem.at[way, p, step],
            device_id=(z_right if way == 0 else z_left, me),
            device_id_type=MESH,
        )

    far = lax.rem(z + S, G)

    def begin(p):
        forward(starts[0][p], p, 0, parts[p].at[piece(p, far)])

    for ft in range(F // FT):
        rows = slice(ft * FT, (ft + 1) * FT)
        for half, part in ((0, part_d0), (1, part_d1)):
            part[rows, :] = (
                jnp.dot(
                    act_t[rows, :],
                    dy[:, half * (D // 2) : (half + 1) * (D // 2)],
                    preferred_element_type=F32,
                )
                * factor
            ).astype(BF16)
    begin(2)
    begin(3)
    for ft in range(F // FT):
        cols = slice(ft * FT, (ft + 1) * FT)
        dact = lax.dot_general(dy[...], wd[cols, :], contract_cols, preferred_element_type=F32)
        dh1[:, cols] = (dact * coef1[:, cols]).astype(BF16)
        dh3[:, cols] = (dact * coef3[:, cols]).astype(BF16)
    for p, part, dh in ((0, part_g, dh1), (1, part_u, dh3)):
        for q in range(4):
            rows = slice(q * Q, (q + 1) * Q)
            part[rows, :] = (
                jnp.dot(xs_t[rows, :], dh[...], preferred_element_type=F32) * factor
            ).astype(BF16)
        begin(p)

    def chunk_at(way, step):
        if way == 0:
            return lax.rem(z + S - step + G, G)
        return lax.rem(z + S + step, G)

    def pass_on(way, p, step):
        ring_copy(way, p, step - 1).wait_recv()
        held = rings[p].at[way, step - 1]
        held[...] = (
            held[...].astype(F32) + parts[p][piece(p, chunk_at(way, step)), :].astype(F32)
        ).astype(BF16)
        forward(way, p, step, held)

    order = ((0, 2), (1, 3), (0, 0), (1, 1), (0, 3), (1, 2), (0, 1), (1, 0))
    for way, p in order:
        if starts[way][p] == 1:
            forward(way, p, 1, parts[p].at[piece(p, chunk_at(way, 1))])
    for way, p in order:
        if starts[way][p] == 0:
            pass_on(way, p, 1)

    for q in range(4):
        rows = slice(q * Q, (q + 1) * Q)
        dx = (
            lax.dot_general(dh1[...], wg[rows, :], contract_cols, preferred_element_type=F32)
            + lax.dot_general(dh3[...], wu[rows, :], contract_cols, preferred_element_type=F32)
        ).astype(BF16)
        for blk in range(NB):
            dx_cat[blk * BR + q * BO : blk * BR + (q + 1) * BO, :] = dx[blk * BO : (blk + 1) * BO]
    for blk in range(NB):
        rows = slice(blk * BR, (blk + 1) * BR)
        send_r[rows, :] = jnp.dot(
            perm_t, dx_cat[rows, :], preferred_element_type=F32
        ).astype(BF16)
    exchange(send_r, got_r, ret_ssem, ret_rsem)
    own_r = keep(send_r, got_r, own_sem.at[2])

    def ring_step(step, carry):
        for way, p in order:
            pass_on(way, p, step)
        return carry

    lax.fori_loop(2, S, ring_step, 0)

    arrived(got_r, ret_rsem, own_r)
    summed = lax.dot_general(onehot[...], got_r[...], contract_rows, preferred_element_type=F32)
    for m in range(2):
        for q in range(4):
            tok_ref[m, :, q * Q : (q + 1) * Q] = summed[
                (q * 2 + m) * T : (q * 2 + m + 1) * T
            ].astype(BF16)

    def finish(p):
        ring_copy(0, p, S - 1).wait_recv()
        ring_copy(1, p, S - 1).wait_recv()
        return (
            rings[p][0, S - 1].astype(F32)
            + rings[p][1, S - 1].astype(F32)
            + parts[p][piece(p, z), :].astype(F32)
        ).astype(BF16)

    down_ref[0, :, 0 : D // 2] = finish(2)
    down_ref[0, :, D // 2 : D] = finish(3)
    gate_ref[0] = finish(0)
    up_ref[0] = finish(1)

    if RW > 1:
        pltpu.make_async_copy(near, near, ids_ssem.at[0]).wait()
    pltpu.make_async_copy(rest, rest, ids_ssem.at[1]).wait()
    for src, sem in ((send_x, fwd_ssem.at[0]), (send_g, fwd_ssem.at[1]), (send_r, ret_ssem)):
        whole = src.at[pl.ds(0, (E - 1) * 16)]
        pltpu.make_async_copy(whole, whole, sem).wait()
    for way in range(2):
        for p in range(4):
            for step in range(starts[way][p], S):
                ring_copy(way, p, step).wait_send()


def settle(*refs):
    number = len(refs) // 2
    sems = refs[-1]
    copies = [
        pltpu.make_async_copy(refs[k], refs[number + k], sems.at[k]) for k in range(number)
    ]
    for copy in copies:
        copy.start()
    for copy in copies:
        copy.wait()


def body(activations, out_grads, chosen_ids, gate_logits, w_gate, w_up, w_down):
    E = lax.axis_size("expert")
    G = lax.axis_size("dp")
    T, D = activations.shape[1:]
    F = w_gate.shape[-1]
    C = chosen_ids.shape[-1]
    Q, S, R4, R16 = D // 4, G // 2, 4 * E, 16 * E
    vmem = pl.BlockSpec(memory_space=pltpu.VMEM)
    hbm = pl.BlockSpec(memory_space=pltpu.HBM)
    V = pltpu.VMEM
    dma = pltpu.SemaphoreType.DMA
    scratch = [
        V((2, 1, 1, C), jnp.int32), V((2, 1, 1, C), jnp.int32),
        V((2, 128), jnp.int32), V((2, 128), jnp.int32),
        V((E, 2, 128), jnp.int32), V((2, E, 128), jnp.int32),
        V((D, F), BF16), V((D, F), BF16), V((F, D), BF16),
        V((8 * T, Q), BF16), V((8 * T, Q), BF16), V((R16, 8 * T), BF16),
        V((R16, Q), BF16), V((R16, Q), BF16), V((R16, Q), BF16), V((R16, Q), BF16),
        V((R4, D), BF16), V((D, R4), BF16), V((R4, D), BF16), V((F, R4), BF16),
        V((R4, F), F32), V((R4, F), F32), V((R4, F), BF16), V((R4, F), BF16), V((R4, 1), F32),
        V((R16, Q), BF16), V((R16, Q), BF16), V((R16, Q), BF16),
        V((D, F), BF16), V((D, F), BF16), V((F, D // 2), BF16), V((F, D // 2), BF16),
        V((2, S, D // G, F), BF16), V((2, S, D // G, F), BF16),
        V((2, S, F // G, D // 2), BF16), V((2, S, F // G, D // 2), BF16),
        dma((3,)), dma((4,)), dma((2,)), dma((2,)), dma((2,)), dma((2,)), dma((3,)), dma, dma,
        dma((2, 4, S)), dma((2, 4, S)),
    ]
    shape = jax.ShapeDtypeStruct
    results = pl.pallas_call(
        functools.partial(fused, (E, G, T, D, F, C)),
        out_shape=(
            shape((2, T, D), BF16),
            shape((1, D // G, F), BF16),
            shape((1, D // G, F), BF16),
            shape((1, F // G, D), BF16),
        ),
        in_specs=[hbm] * 7,
        out_specs=(vmem, vmem, vmem, vmem),
        scratch_shapes=scratch,
        compiler_params=pltpu.CompilerParams(
            collective_id=0, has_side_effects=True, vmem_limit_bytes=533 * 1024 * 1024 // 10
        ),
    )(chosen_ids, gate_logits, activations, out_grads, w_gate, w_up, w_down)
    return pl.pallas_call(
        settle,
        out_shape=tuple(shape(item.shape, item.dtype) for item in results),
        in_specs=[vmem] * 4,
        out_specs=(hbm,) * 4,
        scratch_shapes=[dma((4,))],
        compiler_params=pltpu.CompilerParams(vmem_limit_bytes=16 * 1024 * 1024),
    )(*results)


def solution(mesh):
    placed = (
        P(None, ("dp", "expert"), None),
        P(None, ("dp", "expert"), None),
        P(None, "dp", "expert", None),
        P(None, "dp", "expert", None),
        P("expert", None, None),
        P("expert", None, None),
        P("expert", None, None),
    )
    return jax.shard_map(
        body,
        mesh=mesh,
        in_specs=placed,
        out_specs=(
            P(None, ("dp", "expert"), None),
            P("expert", "dp", None),
            P("expert", "dp", None),
            P("expert", "dp", None),
        ),
        check_vma=False,
    )
```

```python
import functools
import math

import jax
import jax.numpy as jnp
from jax import lax
from jax.experimental import pallas as pl
from jax.experimental.pallas import tpu as pltpu
from jax.sharding import PartitionSpec as P

MESH = pl.DeviceIdType.MESH
BF16 = jnp.bfloat16
F32 = jnp.float32
contract_rows = (((0,), (0,)), ((), ()))
contract_cols = (((1,), (1,)), ((), ()))


def iota(shape, axis):
    return lax.broadcasted_iota(jnp.int32, shape, axis)


def fused(
    sizes,
    ids_hbm, logits_hbm, x_hbm, g_hbm, wg_hbm, wu_hbm, wd_hbm,
    tok_ref, gate_ref, up_ref, down_ref,
    ids_ref, logits_ref, ids_send, logits_pad, ids_all, ids_flat,
    wg, wu, wd,
    xcat, gcat, onehot, send_x, send_g, got_x, got_g,
    xs, xs_t, dy, act_t, coef1, coef3, dh1, dh3, gates,
    dx_cat, send_r, got_r,
    part_g, part_u, part_d0, part_d1,
    ring_g, ring_u, ring_d0, ring_d1,
    w_sem, in_sem, ids_ssem, ids_rsem, fwd_ssem, fwd_rsem, own_sem, ret_ssem, ret_rsem,
    ring_ssem, ring_rsem,
):
    E, G, T, D, F, C = sizes
    Q = D // 4
    S = G // 2
    R4 = 4 * E
    BP = min(16, E)
    BR = BP * 16
    BO = BP * 4
    NB = E // BP
    factor = 1.0 / math.sqrt(G * 2 * C)
    me = lax.axis_index("expert")
    z = lax.axis_index("dp")
    z_right = lax.rem(z + 1, G)
    z_left = lax.rem(z + G - 1, G)

    RW = min(8, E // 2)
    CW = E // RW
    row_at = me // RW
    col_at = lax.rem(me, RW)

    small = [
        pltpu.make_async_copy(src, dst, in_sem.at[k])
        for k, (src, dst) in enumerate(((ids_hbm, ids_ref), (logits_hbm, logits_ref)))
    ]
    for copy in small:
        copy.start()

    def row_mate(k):
        return row_at * RW + lax.rem(col_at + k, RW)

    def col_mate(k):
        return lax.rem(row_at + k, CW) * RW + col_at

    barrier = pltpu.get_barrier_semaphore()
    mates = [(z, row_mate(k)) for k in range(1, RW)] + [(z, col_mate(k)) for k in range(1, CW)]
    for other in mates + [(z_right, me), (z_left, me)]:
        pl.semaphore_signal(barrier, inc=1, device_id=other, device_id_type=MESH)

    for m in range(2):
        for q in range(4):
            rows = pl.ds((q * 2 + m) * T, T)
            pltpu.make_async_copy(
                x_hbm.at[m, :, pl.ds(q * Q, Q)], xcat.at[rows, :], in_sem.at[2]
            ).start()
    for copy in small:
        copy.wait()

    ids_send[...] = jnp.full(ids_send.shape, -1, jnp.int32)
    logits_pad[...] = jnp.zeros(logits_pad.shape, jnp.int32)
    for m in range(2):
        ids_send[m : m + 1, 0:C] = ids_ref[m, 0]
        logits_pad[m : m + 1, 0:C] = logits_ref[m, 0]
    ids_all[pl.ds(me, 1)] = ids_send[...][None]

    pl.semaphore_wait(barrier, RW - 1 + CW - 1 + 2)

    for k in range(1, RW):
        pltpu.make_async_remote_copy(
            src_ref=ids_send,
            dst_ref=ids_all.at[me],
            send_sem=ids_ssem.at[0],
            recv_sem=ids_rsem.at[0],
            device_id=(z, row_mate(k)),
            device_id_type=MESH,
        ).start()
    near = ids_all.at[pl.ds(0, max(RW - 1, 1))]
    if RW > 1:
        pltpu.make_async_copy(near, near, ids_rsem.at[0]).wait()
    ours = ids_all.at[pl.ds(row_at * RW, RW)]
    for k in range(1, CW):
        pltpu.make_async_remote_copy(
            src_ref=ours,
            dst_ref=ours,
            send_sem=ids_ssem.at[1],
            recv_sem=ids_rsem.at[1],
            device_id=(z, col_mate(k)),
            device_id_type=MESH,
        ).start()

    for m in range(2):
        for q in range(4):
            rows = pl.ds((q * 2 + m) * T, T)
            pltpu.make_async_copy(
                g_hbm.at[m, :, pl.ds(q * Q, Q)], gcat.at[rows, :], in_sem.at[3]
            ).start()
    weights = [
        pltpu.make_async_copy(src.at[0], dst, w_sem.at[k])
        for k, (src, dst) in enumerate(((wg_hbm, wg), (wu_hbm, wu), (wd_hbm, wd)))
    ]
    for copy in weights:
        copy.start()

    row = iota((R4, 128), 0)
    micro_row = (row // 2) % 2
    mine = jnp.where(micro_row == 0, ids_send[0:1, :], ids_send[1:2, :]).astype(F32)
    marks = jnp.where(micro_row == 0, logits_pad[0:1, :], logits_pad[1:2, :]).astype(F32)
    low = ((row // 4) * T).astype(F32)
    inside = (mine >= low) & (mine < low + float(T))
    first = jnp.min(jnp.where(inside, mine, 1e6), axis=1, keepdims=True)
    last = jnp.max(jnp.where(inside, mine, -1.0), axis=1, keepdims=True)
    pick = jnp.where(row % 2 == 0, first, last)
    logit = jnp.sum(jnp.where(inside & (mine == pick), marks, 0.0), axis=1, keepdims=True)
    gates[...] = jax.nn.sigmoid(logit * (1.0 / 4096.0))

    rest = ids_all.at[pl.ds(0, (CW - 1) * RW)]
    pltpu.make_async_copy(rest, rest, ids_rsem.at[1]).wait()

    for e in range(E):
        for m in range(2):
            ids_flat[m, e : e + 1, :] = ids_all[e, m : m + 1, :]
    lane = iota((E, 128), 1)
    table = jnp.full((E, 128), -1.0, F32)
    base = (me * T).astype(F32)
    for m in range(2):
        local = ids_flat[m].astype(F32) - base
        inside = (local >= 0.0) & (local < float(T))
        first = jnp.min(jnp.where(inside, local, 1e6), axis=1, keepdims=True)
        last = jnp.max(jnp.where(inside, local, -1.0), axis=1, keepdims=True)
        first_ok = jnp.where(first < 1e5, first, -1.0)
        last_ok = jnp.where(last > first, last, -1.0)
        table = jnp.where(lane == 2 * m, first_ok, table)
        table = jnp.where(lane == 2 * m + 1, last_ok, table)
    table = table.astype(BF16)

    here = pl.ds(pl.multiple_of(me * 16, 16), 16)

    def keep(src, dst, osem):
        own = pltpu.make_async_copy(src.at[here], dst.at[here], osem)
        own.start()
        return own

    def exchange(src, dst, ssem, rsem):
        def one(k, carry):
            peer = lax.rem(me + k, E)
            pltpu.make_async_remote_copy(
                src_ref=src.at[pl.ds(pl.multiple_of(peer * 16, 16), 16)],
                dst_ref=dst.at[here],
                send_sem=ssem,
                recv_sem=rsem,
                device_id=(z, peer),
                device_id_type=MESH,
            ).start()
            return carry

        lax.fori_loop(1, E, one, 0)

    def arrived(dst, rsem, own):
        own.wait()
        whole = dst.at[pl.ds(0, (E - 1) * 16)]
        pltpu.make_async_copy(whole, whole, rsem).wait()

    OB = RW * 16
    line = iota((OB, 1), 0)
    place = (((line // 4) % 4) * (2 * T) + ((line // 2) % 2) * T).astype(F32)
    mine_lane = iota((OB, 128), 1) == iota((OB, 128), 0) % 4
    offsets = [sign * step for step in range(1, CW) for sign in (1, -1)][: CW - 1] + [0]

    def send_row(offset, parity, src, dst, ssem, rsem):
        row = lax.rem(row_at + offset + CW, CW)

        def one(k, carry):
            peer = row * RW + lax.rem(col_at // 2 + k, RW // 2) * 2 + parity
            pltpu.make_async_remote_copy(
                src_ref=src.at[pl.ds(pl.multiple_of(peer * 16, 16), 16)],
                dst_ref=dst.at[here],
                send_sem=ssem,
                recv_sem=rsem,
                device_id=(z, peer),
                device_id_type=MESH,
            ).start()
            return carry

        own = jnp.where(lax.rem(col_at, 2) == parity, 1, 0) if offset == 0 else 0
        lax.fori_loop(own, RW // 2, one, 0)

    pltpu.make_async_copy(xcat, xcat, in_sem.at[2]).wait()
    for offset in offsets:
        row = lax.rem(row_at + offset + CW, CW)
        rows = pl.ds(pl.multiple_of(row * OB, OB), OB)
        spread = (line // 16 + row * RW == iota((OB, E), 1)).astype(F32).astype(BF16)
        values = jnp.dot(spread, table, preferred_element_type=F32)
        chosen = jnp.sum(jnp.where(mine_lane, values, 0.0), axis=1, keepdims=True)
        target = jnp.where(chosen < 0.0, -1.0, chosen + place)
        hot = (iota((OB, 8 * T), 1).astype(F32) == target).astype(F32).astype(BF16)
        onehot[rows, :] = hot
        send_x[rows, :] = jnp.dot(hot, xcat[...], preferred_element_type=F32).astype(BF16)
        send_row(offset, 0, send_x, got_x, fwd_ssem.at[0], fwd_rsem.at[0])
    own_x = keep(send_x, got_x, own_sem.at[0])
    pltpu.make_async_copy(gcat, gcat, in_sem.at[3]).wait()
    for offset in offsets:
        row = lax.rem(row_at + offset + CW, CW)
        rows = pl.ds(pl.multiple_of(row * OB, OB), OB)
        send_g[rows, :] = jnp.dot(
            onehot[rows, :], gcat[...], preferred_element_type=F32
        ).astype(BF16)
        send_row(offset, 0, send_g, got_g, fwd_ssem.at[1], fwd_rsem.at[1])
    for offset in offsets:
        send_row(offset, 1, send_x, got_x, fwd_ssem.at[0], fwd_rsem.at[0])
    for offset in offsets:
        send_row(offset, 1, send_g, got_g, fwd_ssem.at[1], fwd_rsem.at[1])
    own_g = keep(send_g, got_g, own_sem.at[1])

    r = iota((BR, BR), 0)
    c = iota((BR, BR), 1)
    perm = (
        c == ((r // 4) % BP) * 16 + (r // BO) * 4 + r % 4
    ).astype(F32).astype(BF16)
    perm_t = (
        r == ((c // 4) % BP) * 16 + (c // BO) * 4 + c % 4
    ).astype(F32).astype(BF16)

    for copy in weights:
        copy.wait()
    arrived(got_x, fwd_rsem.at[0], own_x)
    for blk in range(NB):
        moved = jnp.dot(perm, got_x[blk * BR : (blk + 1) * BR, :], preferred_element_type=F32)
        for q in range(4):
            xs[blk * BO : (blk + 1) * BO, q * Q : (q + 1) * Q] = moved[
                q * BO : (q + 1) * BO
            ].astype(BF16)
    FT = min(256, F)
    for ft in range(F // FT):
        cols = slice(ft * FT, (ft + 1) * FT)
        h1 = jnp.dot(xs[...], wg[:, cols], preferred_element_type=F32)
        h3 = jnp.dot(xs[...], wu[:, cols], preferred_element_type=F32)
        sig = jax.nn.sigmoid(h1)
        gated = h1 * sig
        act_t[cols, :] = (gated * h3).astype(BF16).T
        coef3[:, cols] = gated
        coef1[:, cols] = h3 * sig * (1.0 + h1 * (1.0 - sig))
    for q in range(4):
        xs_t[q * Q : (q + 1) * Q, :] = xs[:, q * Q : (q + 1) * Q].T

    arrived(got_g, fwd_rsem.at[1], own_g)
    for blk in range(NB):
        moved = jnp.dot(perm, got_g[blk * BR : (blk + 1) * BR, :], preferred_element_type=F32)
        scale = gates[blk * BO : (blk + 1) * BO, :]
        for q in range(4):
            dy[blk * BO : (blk + 1) * BO, q * Q : (q + 1) * Q] = (
                moved[q * BO : (q + 1) * BO] * scale
            ).astype(BF16)

    parts = (part_g, part_u, part_d0, part_d1)
    rings = (ring_g, ring_u, ring_d0, ring_d1)
    heights = (D // G, D // G, F // G, F // G)
    starts = ((0, 1, 0, 1), (1, 0, 1, 0))

    def piece(p, chunk):
        return pl.ds(pl.multiple_of(chunk * heights[p], heights[p]), heights[p])

    def forward(way, p, step, src):
        pltpu.make_async_remote_copy(
            src_ref=src,
            dst_ref=rings[p].at[way, step],
            send_sem=ring_ssem.at[way, p, step],
            recv_sem=ring_rsem.at[way, p, step],
            device_id=(z_right if way == 0 else z_left, me),
            device_id_type=MESH,
        ).start()

    def ring_copy(way, p, step):
        return pltpu.make_async_remote_copy(
            src_ref=rings[p].at[way, step],
            dst_ref=rings[p].at[way, step],
            send_sem=ring_ssem.at[way, p, step],
            recv_sem=ring_rsem.at[way, p, step],
            device_id=(z_right if way == 0 else z_left, me),
            device_id_type=MESH,
        )

    far = lax.rem(z + S, G)

    def begin(p):
        forward(starts[0][p], p, 0, parts[p].at[piece(p, far)])

    for ft in range(F // FT):
        rows = slice(ft * FT, (ft + 1) * FT)
        for half, part in ((0, part_d0), (1, part_d1)):
            part[rows, :] = (
                jnp.dot(
                    act_t[rows, :],
                    dy[:, half * (D // 2) : (half + 1) * (D // 2)],
                    preferred_element_type=F32,
                )
                * factor
            ).astype(BF16)
    begin(2)
    begin(3)
    for ft in range(F // FT):
        cols = slice(ft * FT, (ft + 1) * FT)
        dact = lax.dot_general(dy[...], wd[cols, :], contract_cols, preferred_element_type=F32)
        dh1[:, cols] = (dact * coef1[:, cols]).astype(BF16)
        dh3[:, cols] = (dact * coef3[:, cols]).astype(BF16)
    for p, part, dh in ((0, part_g, dh1), (1, part_u, dh3)):
        for q in range(4):
            rows = slice(q * Q, (q + 1) * Q)
            part[rows, :] = (
                jnp.dot(xs_t[rows, :], dh[...], preferred_element_type=F32) * factor
            ).astype(BF16)
        begin(p)

    def chunk_at(way, step):
        if way == 0:
            return lax.rem(z + S - step + G, G)
        return lax.rem(z + S + step, G)

    def pass_on(way, p, step):
        ring_copy(way, p, step - 1).wait_recv()
        held = rings[p].at[way, step - 1]
        held[...] = (
            held[...].astype(F32) + parts[p][piece(p, chunk_at(way, step)), :].astype(F32)
        ).astype(BF16)
        forward(way, p, step, held)

    order = ((0, 2), (1, 3), (0, 0), (1, 1), (0, 3), (1, 2), (0, 1), (1, 0))
    for way, p in order:
        if starts[way][p] == 1:
            forward(way, p, 1, parts[p].at[piece(p, chunk_at(way, 1))])
    for way, p in order:
        if starts[way][p] == 0:
            pass_on(way, p, 1)

    for q in range(4):
        rows = slice(q * Q, (q + 1) * Q)
        dx = (
            lax.dot_general(dh1[...], wg[rows, :], contract_cols, preferred_element_type=F32)
            + lax.dot_general(dh3[...], wu[rows, :], contract_cols, preferred_element_type=F32)
        ).astype(BF16)
        for blk in range(NB):
            dx_cat[blk * BR + q * BO : blk * BR + (q + 1) * BO, :] = dx[blk * BO : (blk + 1) * BO]
    for blk in range(NB):
        rows = slice(blk * BR, (blk + 1) * BR)
        send_r[rows, :] = jnp.dot(
            perm_t, dx_cat[rows, :], preferred_element_type=F32
        ).astype(BF16)
    exchange(send_r, got_r, ret_ssem, ret_rsem)
    own_r = keep(send_r, got_r, own_sem.at[2])

    def ring_step(step, carry):
        for way, p in order:
            pass_on(way, p, step)
        return carry

    lax.fori_loop(2, S, ring_step, 0)

    arrived(got_r, ret_rsem, own_r)
    summed = lax.dot_general(onehot[...], got_r[...], contract_rows, preferred_element_type=F32)
    for m in range(2):
        for q in range(4):
            tok_ref[m, :, q * Q : (q + 1) * Q] = summed[
                (q * 2 + m) * T : (q * 2 + m + 1) * T
            ].astype(BF16)

    def finish(p):
        ring_copy(0, p, S - 1).wait_recv()
        ring_copy(1, p, S - 1).wait_recv()
        return (
            rings[p][0, S - 1].astype(F32)
            + rings[p][1, S - 1].astype(F32)
            + parts[p][piece(p, z), :].astype(F32)
        ).astype(BF16)

    down_ref[0, :, 0 : D // 2] = finish(2)
    down_ref[0, :, D // 2 : D] = finish(3)
    gate_ref[0] = finish(0)
    up_ref[0] = finish(1)

    if RW > 1:
        pltpu.make_async_copy(near, near, ids_ssem.at[0]).wait()
    pltpu.make_async_copy(rest, rest, ids_ssem.at[1]).wait()
    for src, sem in ((send_x, fwd_ssem.at[0]), (send_g, fwd_ssem.at[1]), (send_r, ret_ssem)):
        whole = src.at[pl.ds(0, (E - 1) * 16)]
        pltpu.make_async_copy(whole, whole, sem).wait()
    for way in range(2):
        for p in range(4):
            for step in range(starts[way][p], S):
                ring_copy(way, p, step).wait_send()


def settle(*refs):
    number = len(refs) // 2
    sems = refs[-1]
    copies = [
        pltpu.make_async_copy(refs[k], refs[number + k], sems.at[k]) for k in range(number)
    ]
    for copy in copies:
        copy.start()
    for copy in copies:
        copy.wait()


def body(activations, out_grads, chosen_ids, gate_logits, w_gate, w_up, w_down):
    E = lax.axis_size("expert")
    G = lax.axis_size("dp")
    T, D = activations.shape[1:]
    F = w_gate.shape[-1]
    C = chosen_ids.shape[-1]
    Q, S, R4, R16 = D // 4, G // 2, 4 * E, 16 * E
    vmem = pl.BlockSpec(memory_space=pltpu.VMEM)
    hbm = pl.BlockSpec(memory_space=pltpu.HBM)
    V = pltpu.VMEM
    dma = pltpu.SemaphoreType.DMA
    scratch = [
        V((2, 1, 1, C), jnp.int32), V((2, 1, 1, C), jnp.int32),
        V((2, 128), jnp.int32), V((2, 128), jnp.int32),
        V((E, 2, 128), jnp.int32), V((2, E, 128), jnp.int32),
        V((D, F), BF16), V((D, F), BF16), V((F, D), BF16),
        V((8 * T, Q), BF16), V((8 * T, Q), BF16), V((R16, 8 * T), BF16),
        V((R16, Q), BF16), V((R16, Q), BF16), V((R16, Q), BF16), V((R16, Q), BF16),
        V((R4, D), BF16), V((D, R4), BF16), V((R4, D), BF16), V((F, R4), BF16),
        V((R4, F), F32), V((R4, F), F32), V((R4, F), BF16), V((R4, F), BF16), V((R4, 1), F32),
        V((R16, Q), BF16), V((R16, Q), BF16), V((R16, Q), BF16),
        V((D, F), BF16), V((D, F), BF16), V((F, D // 2), BF16), V((F, D // 2), BF16),
        V((2, S, D // G, F), BF16), V((2, S, D // G, F), BF16),
        V((2, S, F // G, D // 2), BF16), V((2, S, F // G, D // 2), BF16),
        dma((3,)), dma((4,)), dma((2,)), dma((2,)), dma((2,)), dma((2,)), dma((3,)), dma, dma,
        dma((2, 4, S)), dma((2, 4, S)),
    ]
    shape = jax.ShapeDtypeStruct
    results = pl.pallas_call(
        functools.partial(fused, (E, G, T, D, F, C)),
        out_shape=(
            shape((2, T, D), BF16),
            shape((1, D // G, F), BF16),
            shape((1, D // G, F), BF16),
            shape((1, F // G, D), BF16),
        ),
        in_specs=[hbm] * 7,
        out_specs=(vmem, vmem, vmem, vmem),
        scratch_shapes=scratch,
        compiler_params=pltpu.CompilerParams(
            collective_id=0, has_side_effects=True, vmem_limit_bytes=533 * 1024 * 1024 // 10
        ),
    )(chosen_ids, gate_logits, activations, out_grads, w_gate, w_up, w_down)
    return pl.pallas_call(
        settle,
        out_shape=tuple(shape(item.shape, item.dtype) for item in results),
        in_specs=[vmem] * 4,
        out_specs=(hbm,) * 4,
        scratch_shapes=[dma((4,))],
        compiler_params=pltpu.CompilerParams(vmem_limit_bytes=16 * 1024 * 1024),
    )(*results)


def solution(mesh):
    placed = (
        P(None, ("dp", "expert"), None),
        P(None, ("dp", "expert"), None),
        P(None, "dp", "expert", None),
        P(None, "dp", "expert", None),
        P("expert", None, None),
        P("expert", None, None),
        P("expert", None, None),
    )
    return jax.shard_map(
        body,
        mesh=mesh,
        in_specs=placed,
        out_specs=(
            P(None, ("dp", "expert"), None),
            P("expert", "dp", None),
            P("expert", "dp", None),
            P("expert", "dp", None),
        ),
        check_vma=False,
    )
```

```python
import functools
import math

import jax
import jax.numpy as jnp
from jax import lax
from jax.experimental import pallas as pl
from jax.experimental.pallas import tpu as pltpu
from jax.sharding import PartitionSpec as P

MESH = pl.DeviceIdType.MESH
BF16 = jnp.bfloat16
F32 = jnp.float32
contract_rows = (((0,), (0,)), ((), ()))
contract_cols = (((1,), (1,)), ((), ()))


def iota(shape, axis):
    return lax.broadcasted_iota(jnp.int32, shape, axis)


def fused(
    sizes,
    ids_hbm, logits_hbm, x_hbm, g_hbm, wg_hbm, wu_hbm, wd_hbm,
    tok_ref, gate_ref, up_ref, down_ref,
    ids_ref, logits_ref, ids_send, logits_pad, ids_all, ids_flat,
    wg, wu, wd,
    xcat, gcat, onehot, send_x, send_g, got_x, got_g,
    xs, xs_t, dy, act_t, coef1, coef3, dh1, dh3, gates,
    dx_cat, send_r, got_r,
    part_g, part_u, part_d0, part_d1,
    ring_g, ring_u, ring_d0, ring_d1,
    w_sem, in_sem, ids_ssem, ids_rsem, fwd_ssem, fwd_rsem, own_sem, ret_ssem, ret_rsem,
    ring_ssem, ring_rsem,
):
    E, G, T, D, F, C = sizes
    Q = D // 4
    S = G // 2
    R4 = 4 * E
    BP = min(16, E)
    BR = BP * 16
    BO = BP * 4
    NB = E // BP
    factor = 1.0 / math.sqrt(G * 2 * C)
    me = lax.axis_index("expert")
    z = lax.axis_index("dp")
    z_right = lax.rem(z + 1, G)
    z_left = lax.rem(z + G - 1, G)

    RW = min(8, E // 2)
    CW = E // RW
    row_at = me // RW
    col_at = lax.rem(me, RW)

    small = [
        pltpu.make_async_copy(src, dst, in_sem.at[k])
        for k, (src, dst) in enumerate(((ids_hbm, ids_ref), (logits_hbm, logits_ref)))
    ]
    for copy in small:
        copy.start()

    def row_mate(k):
        return row_at * RW + lax.rem(col_at + k, RW)

    def col_mate(k):
        return lax.rem(row_at + k, CW) * RW + col_at

    barrier = pltpu.get_barrier_semaphore()
    mates = [(z, row_mate(k)) for k in range(1, RW)] + [(z, col_mate(k)) for k in range(1, CW)]
    for other in mates + [(z_right, me), (z_left, me)]:
        pl.semaphore_signal(barrier, inc=1, device_id=other, device_id_type=MESH)

    for m in range(2):
        for q in range(4):
            rows = pl.ds((q * 2 + m) * T, T)
            pltpu.make_async_copy(
                x_hbm.at[m, :, pl.ds(q * Q, Q)], xcat.at[rows, :], in_sem.at[2]
            ).start()
    for copy in small:
        copy.wait()

    ids_send[...] = jnp.full(ids_send.shape, -1, jnp.int32)
    logits_pad[...] = jnp.zeros(logits_pad.shape, jnp.int32)
    for m in range(2):
        ids_send[m : m + 1, 0:C] = ids_ref[m, 0]
        logits_pad[m : m + 1, 0:C] = logits_ref[m, 0]
    ids_all[pl.ds(me, 1)] = ids_send[...][None]

    pl.semaphore_wait(barrier, RW - 1 + CW - 1 + 2)

    for k in range(1, RW):
        pltpu.make_async_remote_copy(
            src_ref=ids_send,
            dst_ref=ids_all.at[me],
            send_sem=ids_ssem.at[0],
            recv_sem=ids_rsem.at[0],
            device_id=(z, row_mate(k)),
            device_id_type=MESH,
        ).start()
    near = ids_all.at[pl.ds(0, max(RW - 1, 1))]
    if RW > 1:
        pltpu.make_async_copy(near, near, ids_rsem.at[0]).wait()
    ours = ids_all.at[pl.ds(row_at * RW, RW)]
    for k in range(1, CW):
        pltpu.make_async_remote_copy(
            src_ref=ours,
            dst_ref=ours,
            send_sem=ids_ssem.at[1],
            recv_sem=ids_rsem.at[1 + row_at],
            device_id=(z, col_mate(k)),
            device_id_type=MESH,
        ).start()

    for m in range(2):
        for q in range(4):
            rows = pl.ds((q * 2 + m) * T, T)
            pltpu.make_async_copy(
                g_hbm.at[m, :, pl.ds(q * Q, Q)], gcat.at[rows, :], in_sem.at[3]
            ).start()
    weights = [
        pltpu.make_async_copy(src.at[0], dst, w_sem.at[k])
        for k, (src, dst) in enumerate(((wg_hbm, wg), (wu_hbm, wu), (wd_hbm, wd)))
    ]
    for copy in weights:
        copy.start()

    row = iota((R4, 128), 0)
    micro_row = (row // 2) % 2
    mine = jnp.where(micro_row == 0, ids_send[0:1, :], ids_send[1:2, :]).astype(F32)
    marks = jnp.where(micro_row == 0, logits_pad[0:1, :], logits_pad[1:2, :]).astype(F32)
    low = ((row // 4) * T).astype(F32)
    inside = (mine >= low) & (mine < low + float(T))
    first = jnp.min(jnp.where(inside, mine, 1e6), axis=1, keepdims=True)
    last = jnp.max(jnp.where(inside, mine, -1.0), axis=1, keepdims=True)
    pick = jnp.where(row % 2 == 0, first, last)
    logit = jnp.sum(jnp.where(inside & (mine == pick), marks, 0.0), axis=1, keepdims=True)
    gates[...] = jax.nn.sigmoid(logit * (1.0 / 4096.0))

    rest = ids_all.at[pl.ds(0, (CW - 1) * RW)]

    lane = iota((RW, 128), 1)
    base = (me * T).astype(F32)

    def wanted(row):
        table = jnp.full((RW, 128), -1.0, F32)
        for m in range(2):
            for i in range(RW):
                ids_flat[m, i : i + 1, :] = ids_all[row * RW + i, m : m + 1, :]
            local = ids_flat[m].astype(F32) - base
            inside = (local >= 0.0) & (local < float(T))
            first = jnp.min(jnp.where(inside, local, 1e6), axis=1, keepdims=True)
            last = jnp.max(jnp.where(inside, local, -1.0), axis=1, keepdims=True)
            first_ok = jnp.where(first < 1e5, first, -1.0)
            last_ok = jnp.where(last > first, last, -1.0)
            table = jnp.where(lane == 2 * m, first_ok, table)
            table = jnp.where(lane == 2 * m + 1, last_ok, table)
        return table

    here = pl.ds(pl.multiple_of(me * 16, 16), 16)

    def keep(src, dst, osem):
        own = pltpu.make_async_copy(src.at[here], dst.at[here], osem)
        own.start()
        return own

    def exchange(src, dst, ssem, rsem):
        def one(k, carry):
            peer = lax.rem(me + k, E)
            pltpu.make_async_remote_copy(
                src_ref=src.at[pl.ds(pl.multiple_of(peer * 16, 16), 16)],
                dst_ref=dst.at[here],
                send_sem=ssem,
                recv_sem=rsem,
                device_id=(z, peer),
                device_id_type=MESH,
            ).start()
            return carry

        lax.fori_loop(1, E, one, 0)

    def arrived(dst, rsem, own):
        own.wait()
        whole = dst.at[pl.ds(0, (E - 1) * 16)]
        pltpu.make_async_copy(whole, whole, rsem).wait()

    OB = RW * 16
    line = iota((OB, 1), 0)
    place = (((line // 4) % 4) * (2 * T) + ((line // 2) % 2) * T).astype(F32)
    spread = (line // 16 == iota((OB, RW), 1)).astype(F32)
    mine_lane = iota((OB, 128), 1) == iota((OB, 128), 0) % 4
    offsets = [sign * step for step in range(1, CW) for sign in (1, -1)][: CW - 1]
    offsets = [0] + offsets

    def send_row(offset, parity, src, dst, ssem, rsem):
        row = lax.rem(row_at + offset + CW, CW)

        def one(k, carry):
            peer = row * RW + lax.rem(col_at // 2 + k, RW // 2) * 2 + parity
            pltpu.make_async_remote_copy(
                src_ref=src.at[pl.ds(pl.multiple_of(peer * 16, 16), 16)],
                dst_ref=dst.at[here],
                send_sem=ssem,
                recv_sem=rsem,
                device_id=(z, peer),
                device_id_type=MESH,
            ).start()
            return carry

        own = jnp.where(lax.rem(col_at, 2) == parity, 1, 0) if offset == 0 else 0
        lax.fori_loop(own, RW // 2, one, 0)

    pltpu.make_async_copy(xcat, xcat, in_sem.at[2]).wait()
    for offset in offsets:
        row = lax.rem(row_at + offset + CW, CW)
        rows = pl.ds(pl.multiple_of(row * OB, OB), OB)
        if offset:
            theirs = ids_all.at[pl.ds(row * RW, RW)]
            pltpu.make_async_copy(theirs, theirs, ids_rsem.at[1 + row]).wait()
        values = jnp.dot(spread, wanted(row), preferred_element_type=F32)
        chosen = jnp.sum(jnp.where(mine_lane, values, 0.0), axis=1, keepdims=True)
        target = jnp.where(chosen < 0.0, -1.0, chosen + place)
        hot = (iota((OB, 8 * T), 1).astype(F32) == target).astype(F32).astype(BF16)
        onehot[rows, :] = hot
        send_x[rows, :] = jnp.dot(hot, xcat[...], preferred_element_type=F32).astype(BF16)
        send_row(offset, 0, send_x, got_x, fwd_ssem.at[0], fwd_rsem.at[0])
    own_x = keep(send_x, got_x, own_sem.at[0])
    pltpu.make_async_copy(gcat, gcat, in_sem.at[3]).wait()
    for offset in offsets:
        row = lax.rem(row_at + offset + CW, CW)
        rows = pl.ds(pl.multiple_of(row * OB, OB), OB)
        send_g[rows, :] = jnp.dot(
            onehot[rows, :], gcat[...], preferred_element_type=F32
        ).astype(BF16)
        send_row(offset, 0, send_g, got_g, fwd_ssem.at[1], fwd_rsem.at[1])
    for offset in offsets:
        send_row(offset, 1, send_x, got_x, fwd_ssem.at[0], fwd_rsem.at[0])
    for offset in offsets:
        send_row(offset, 1, send_g, got_g, fwd_ssem.at[1], fwd_rsem.at[1])
    own_g = keep(send_g, got_g, own_sem.at[1])

    r = iota((BR, BR), 0)
    c = iota((BR, BR), 1)
    perm = (
        c == ((r // 4) % BP) * 16 + (r // BO) * 4 + r % 4
    ).astype(F32).astype(BF16)
    perm_t = (
        r == ((c // 4) % BP) * 16 + (c // BO) * 4 + c % 4
    ).astype(F32).astype(BF16)

    for copy in weights:
        copy.wait()
    arrived(got_x, fwd_rsem.at[0], own_x)
    for blk in range(NB):
        moved = jnp.dot(perm, got_x[blk * BR : (blk + 1) * BR, :], preferred_element_type=F32)
        for q in range(4):
            xs[blk * BO : (blk + 1) * BO, q * Q : (q + 1) * Q] = moved[
                q * BO : (q + 1) * BO
            ].astype(BF16)
    FT = min(256, F)
    for ft in range(F // FT):
        cols = slice(ft * FT, (ft + 1) * FT)
        h1 = jnp.dot(xs[...], wg[:, cols], preferred_element_type=F32)
        h3 = jnp.dot(xs[...], wu[:, cols], preferred_element_type=F32)
        sig = jax.nn.sigmoid(h1)
        gated = h1 * sig
        act_t[cols, :] = (gated * h3).astype(BF16).T
        coef3[:, cols] = gated
        coef1[:, cols] = h3 * sig * (1.0 + h1 * (1.0 - sig))
    for q in range(4):
        xs_t[q * Q : (q + 1) * Q, :] = xs[:, q * Q : (q + 1) * Q].T

    arrived(got_g, fwd_rsem.at[1], own_g)
    for blk in range(NB):
        moved = jnp.dot(perm, got_g[blk * BR : (blk + 1) * BR, :], preferred_element_type=F32)
        scale = gates[blk * BO : (blk + 1) * BO, :]
        for q in range(4):
            dy[blk * BO : (blk + 1) * BO, q * Q : (q + 1) * Q] = (
                moved[q * BO : (q + 1) * BO] * scale
            ).astype(BF16)

    parts = (part_g, part_u, part_d0, part_d1)
    rings = (ring_g, ring_u, ring_d0, ring_d1)
    heights = (D // G, D // G, F // G, F // G)
    starts = ((0, 1, 0, 1), (1, 0, 1, 0))

    def piece(p, chunk):
        return pl.ds(pl.multiple_of(chunk * heights[p], heights[p]), heights[p])

    def forward(way, p, step, src):
        pltpu.make_async_remote_copy(
            src_ref=src,
            dst_ref=rings[p].at[way, step],
            send_sem=ring_ssem.at[way, p, step],
            recv_sem=ring_rsem.at[way, p, step],
            device_id=(z_right if way == 0 else z_left, me),
            device_id_type=MESH,
        ).start()

    def ring_copy(way, p, step):
        return pltpu.make_async_remote_copy(
            src_ref=rings[p].at[way, step],
            dst_ref=rings[p].at[way, step],
            send_sem=ring_ssem.at[way, p, step],
            recv_sem=ring_rsem.at[way, p, step],
            device_id=(z_right if way == 0 else z_left, me),
            device_id_type=MESH,
        )

    far = lax.rem(z + S, G)

    def begin(p):
        forward(starts[0][p], p, 0, parts[p].at[piece(p, far)])

    for ft in range(F // FT):
        rows = slice(ft * FT, (ft + 1) * FT)
        for half, part in ((0, part_d0), (1, part_d1)):
            part[rows, :] = (
                jnp.dot(
                    act_t[rows, :],
                    dy[:, half * (D // 2) : (half + 1) * (D // 2)],
                    preferred_element_type=F32,
                )
                * factor
            ).astype(BF16)
    begin(2)
    begin(3)
    for ft in range(F // FT):
        cols = slice(ft * FT, (ft + 1) * FT)
        dact = lax.dot_general(dy[...], wd[cols, :], contract_cols, preferred_element_type=F32)
        dh1[:, cols] = (dact * coef1[:, cols]).astype(BF16)
        dh3[:, cols] = (dact * coef3[:, cols]).astype(BF16)
    for p, part, dh in ((0, part_g, dh1), (1, part_u, dh3)):
        for q in range(4):
            rows = slice(q * Q, (q + 1) * Q)
            part[rows, :] = (
                jnp.dot(xs_t[rows, :], dh[...], preferred_element_type=F32) * factor
            ).astype(BF16)
        begin(p)

    def chunk_at(way, step):
        if way == 0:
            return lax.rem(z + S - step + G, G)
        return lax.rem(z + S + step, G)

    def pass_on(way, p, step):
        ring_copy(way, p, step - 1).wait_recv()
        held = rings[p].at[way, step - 1]
        held[...] = (
            held[...].astype(F32) + parts[p][piece(p, chunk_at(way, step)), :].astype(F32)
        ).astype(BF16)
        forward(way, p, step, held)

    order = ((0, 2), (1, 3), (0, 0), (1, 1), (0, 3), (1, 2), (0, 1), (1, 0))
    for way, p in order:
        if starts[way][p] == 1:
            forward(way, p, 1, parts[p].at[piece(p, chunk_at(way, 1))])
    for way, p in order:
        if starts[way][p] == 0:
            pass_on(way, p, 1)

    for q in range(4):
        rows = slice(q * Q, (q + 1) * Q)
        dx = (
            lax.dot_general(dh1[...], wg[rows, :], contract_cols, preferred_element_type=F32)
            + lax.dot_general(dh3[...], wu[rows, :], contract_cols, preferred_element_type=F32)
        ).astype(BF16)
        for blk in range(NB):
            dx_cat[blk * BR + q * BO : blk * BR + (q + 1) * BO, :] = dx[blk * BO : (blk + 1) * BO]
    for blk in range(NB):
        rows = slice(blk * BR, (blk + 1) * BR)
        send_r[rows, :] = jnp.dot(
            perm_t, dx_cat[rows, :], preferred_element_type=F32
        ).astype(BF16)
    exchange(send_r, got_r, ret_ssem, ret_rsem)
    own_r = keep(send_r, got_r, own_sem.at[2])

    def ring_step(step, carry):
        for way, p in order:
            pass_on(way, p, step)
        return carry

    lax.fori_loop(2, S, ring_step, 0)

    arrived(got_r, ret_rsem, own_r)
    summed = lax.dot_general(onehot[...], got_r[...], contract_rows, preferred_element_type=F32)
    for m in range(2):
        for q in range(4):
            tok_ref[m, :, q * Q : (q + 1) * Q] = summed[
                (q * 2 + m) * T : (q * 2 + m + 1) * T
            ].astype(BF16)

    def finish(p):
        ring_copy(0, p, S - 1).wait_recv()
        ring_copy(1, p, S - 1).wait_recv()
        return (
            rings[p][0, S - 1].astype(F32)
            + rings[p][1, S - 1].astype(F32)
            + parts[p][piece(p, z), :].astype(F32)
        ).astype(BF16)

    down_ref[0, :, 0 : D // 2] = finish(2)
    down_ref[0, :, D // 2 : D] = finish(3)
    gate_ref[0] = finish(0)
    up_ref[0] = finish(1)

    if RW > 1:
        pltpu.make_async_copy(near, near, ids_ssem.at[0]).wait()
    pltpu.make_async_copy(rest, rest, ids_ssem.at[1]).wait()
    for src, sem in ((send_x, fwd_ssem.at[0]), (send_g, fwd_ssem.at[1]), (send_r, ret_ssem)):
        whole = src.at[pl.ds(0, (E - 1) * 16)]
        pltpu.make_async_copy(whole, whole, sem).wait()
    for way in range(2):
        for p in range(4):
            for step in range(starts[way][p], S):
                ring_copy(way, p, step).wait_send()


def settle(*refs):
    number = len(refs) // 2
    sems = refs[-1]
    copies = [
        pltpu.make_async_copy(refs[k], refs[number + k], sems.at[k]) for k in range(number)
    ]
    for copy in copies:
        copy.start()
    for copy in copies:
        copy.wait()


def body(activations, out_grads, chosen_ids, gate_logits, w_gate, w_up, w_down):
    E = lax.axis_size("expert")
    G = lax.axis_size("dp")
    T, D = activations.shape[1:]
    F = w_gate.shape[-1]
    C = chosen_ids.shape[-1]
    Q, S, R4, R16 = D // 4, G // 2, 4 * E, 16 * E
    RW = min(8, E // 2)
    vmem = pl.BlockSpec(memory_space=pltpu.VMEM)
    hbm = pl.BlockSpec(memory_space=pltpu.HBM)
    V = pltpu.VMEM
    dma = pltpu.SemaphoreType.DMA
    scratch = [
        V((2, 1, 1, C), jnp.int32), V((2, 1, 1, C), jnp.int32),
        V((2, 128), jnp.int32), V((2, 128), jnp.int32),
        V((E, 2, 128), jnp.int32), V((2, RW, 128), jnp.int32),
        V((D, F), BF16), V((D, F), BF16), V((F, D), BF16),
        V((8 * T, Q), BF16), V((8 * T, Q), BF16), V((R16, 8 * T), BF16),
        V((R16, Q), BF16), V((R16, Q), BF16), V((R16, Q), BF16), V((R16, Q), BF16),
        V((R4, D), BF16), V((D, R4), BF16), V((R4, D), BF16), V((F, R4), BF16),
        V((R4, F), F32), V((R4, F), F32), V((R4, F), BF16), V((R4, F), BF16), V((R4, 1), F32),
        V((R16, Q), BF16), V((R16, Q), BF16), V((R16, Q), BF16),
        V((D, F), BF16), V((D, F), BF16), V((F, D // 2), BF16), V((F, D // 2), BF16),
        V((2, S, D // G, F), BF16), V((2, S, D // G, F), BF16),
        V((2, S, F // G, D // 2), BF16), V((2, S, F // G, D // 2), BF16),
        dma((3,)), dma((4,)), dma((2,)), dma((1 + E // RW,)), dma((2,)), dma((2,)), dma((3,)), dma, dma,
        dma((2, 4, S)), dma((2, 4, S)),
    ]
    shape = jax.ShapeDtypeStruct
    results = pl.pallas_call(
        functools.partial(fused, (E, G, T, D, F, C)),
        out_shape=(
            shape((2, T, D), BF16),
            shape((1, D // G, F), BF16),
            shape((1, D // G, F), BF16),
            shape((1, F // G, D), BF16),
        ),
        in_specs=[hbm] * 7,
        out_specs=(vmem, vmem, vmem, vmem),
        scratch_shapes=scratch,
        compiler_params=pltpu.CompilerParams(
            collective_id=0, has_side_effects=True, vmem_limit_bytes=533 * 1024 * 1024 // 10
        ),
    )(chosen_ids, gate_logits, activations, out_grads, w_gate, w_up, w_down)
    return pl.pallas_call(
        settle,
        out_shape=tuple(shape(item.shape, item.dtype) for item in results),
        in_specs=[vmem] * 4,
        out_specs=(hbm,) * 4,
        scratch_shapes=[dma((4,))],
        compiler_params=pltpu.CompilerParams(vmem_limit_bytes=16 * 1024 * 1024),
    )(*results)


def solution(mesh):
    placed = (
        P(None, ("dp", "expert"), None),
        P(None, ("dp", "expert"), None),
        P(None, "dp", "expert", None),
        P(None, "dp", "expert", None),
        P("expert", None, None),
        P("expert", None, None),
        P("expert", None, None),
    )
    return jax.shard_map(
        body,
        mesh=mesh,
        in_specs=placed,
        out_specs=(
            P(None, ("dp", "expert"), None),
            P("expert", "dp", None),
            P("expert", "dp", None),
            P("expert", "dp", None),
        ),
        check_vma=False,
    )
```

```python
import functools
import math

import jax
import jax.numpy as jnp
from jax import lax
from jax.experimental import pallas as pl
from jax.experimental.pallas import tpu as pltpu
from jax.sharding import PartitionSpec as P

MESH = pl.DeviceIdType.MESH
BF16 = jnp.bfloat16
F32 = jnp.float32
contract_rows = (((0,), (0,)), ((), ()))
contract_cols = (((1,), (1,)), ((), ()))


def iota(shape, axis):
    return lax.broadcasted_iota(jnp.int32, shape, axis)


def fused(
    sizes,
    ids_hbm, logits_hbm, x_hbm, g_hbm, wg_hbm, wu_hbm, wd_hbm,
    tok_ref, gate_ref, up_ref, down_ref,
    ids_ref, logits_ref, ids_send, logits_pad, ids_all, ids_flat,
    wg, wu, wd,
    xcat, gcat, onehot, send_x, send_g, got_x, got_g,
    xs, xs_t, dy, act_t, coef1, coef3, dh1, dh3, gates,
    dx_cat, send_r, got_r,
    part_g, part_u, part_d0, part_d1,
    ring_g, ring_u, ring_d0, ring_d1,
    w_sem, in_sem, ids_ssem, ids_rsem, fwd_ssem, fwd_rsem, own_sem, ret_ssem, ret_rsem,
    ring_ssem, ring_rsem,
):
    E, G, T, D, F, C = sizes
    Q = D // 4
    S = G // 2
    R4 = 4 * E
    BP = min(16, E)
    BR = BP * 16
    BO = BP * 4
    NB = E // BP
    factor = 1.0 / math.sqrt(G * 2 * C)
    me = lax.axis_index("expert")
    z = lax.axis_index("dp")
    z_right = lax.rem(z + 1, G)
    z_left = lax.rem(z + G - 1, G)

    RW = min(8, E // 2)
    CW = E // RW
    row_at = me // RW
    col_at = lax.rem(me, RW)

    small = [
        pltpu.make_async_copy(src, dst, in_sem.at[k])
        for k, (src, dst) in enumerate(((ids_hbm, ids_ref), (logits_hbm, logits_ref)))
    ]
    for copy in small:
        copy.start()

    def row_mate(k):
        return row_at * RW + lax.rem(col_at + k, RW)

    def col_mate(k):
        return lax.rem(row_at + k, CW) * RW + col_at

    barrier = pltpu.get_barrier_semaphore()
    mates = [(z, row_mate(k)) for k in range(1, RW)] + [(z, col_mate(k)) for k in range(1, CW)]
    for other in mates + [(z_right, me), (z_left, me)]:
        pl.semaphore_signal(barrier, inc=1, device_id=other, device_id_type=MESH)

    for m in range(2):
        for q in range(4):
            rows = pl.ds((q * 2 + m) * T, T)
            pltpu.make_async_copy(
                x_hbm.at[m, :, pl.ds(q * Q, Q)], xcat.at[rows, :], in_sem.at[2]
            ).start()
    for copy in small:
        copy.wait()

    ids_send[...] = jnp.full(ids_send.shape, -1, jnp.int32)
    logits_pad[...] = jnp.zeros(logits_pad.shape, jnp.int32)
    for m in range(2):
        ids_send[m : m + 1, 0:C] = ids_ref[m, 0]
        logits_pad[m : m + 1, 0:C] = logits_ref[m, 0]
    ids_all[pl.ds(me, 1)] = ids_send[...][None]

    pl.semaphore_wait(barrier, RW - 1 + CW - 1 + 2)

    for k in range(1, RW):
        pltpu.make_async_remote_copy(
            src_ref=ids_send,
            dst_ref=ids_all.at[me],
            send_sem=ids_ssem.at[0],
            recv_sem=ids_rsem.at[0],
            device_id=(z, row_mate(k)),
            device_id_type=MESH,
        ).start()
    near = ids_all.at[pl.ds(0, max(RW - 1, 1))]
    if RW > 1:
        pltpu.make_async_copy(near, near, ids_rsem.at[0]).wait()
    ours = ids_all.at[pl.ds(row_at * RW, RW)]
    for k in range(1, CW):
        pltpu.make_async_remote_copy(
            src_ref=ours,
            dst_ref=ours,
            send_sem=ids_ssem.at[1],
            recv_sem=ids_rsem.at[1 + row_at],
            device_id=(z, col_mate(k)),
            device_id_type=MESH,
        ).start()

    for m in range(2):
        for q in range(4):
            rows = pl.ds((q * 2 + m) * T, T)
            pltpu.make_async_copy(
                g_hbm.at[m, :, pl.ds(q * Q, Q)], gcat.at[rows, :], in_sem.at[3]
            ).start()
    weights = [
        pltpu.make_async_copy(src.at[0], dst, w_sem.at[k])
        for k, (src, dst) in enumerate(((wg_hbm, wg), (wu_hbm, wu), (wd_hbm, wd)))
    ]
    for copy in weights:
        copy.start()

    row = iota((R4, 128), 0)
    micro_row = (row // 2) % 2
    mine = jnp.where(micro_row == 0, ids_send[0:1, :], ids_send[1:2, :]).astype(F32)
    marks = jnp.where(micro_row == 0, logits_pad[0:1, :], logits_pad[1:2, :]).astype(F32)
    low = ((row // 4) * T).astype(F32)
    inside = (mine >= low) & (mine < low + float(T))
    first = jnp.min(jnp.where(inside, mine, 1e6), axis=1, keepdims=True)
    last = jnp.max(jnp.where(inside, mine, -1.0), axis=1, keepdims=True)
    pick = jnp.where(row % 2 == 0, first, last)
    logit = jnp.sum(jnp.where(inside & (mine == pick), marks, 0.0), axis=1, keepdims=True)
    gates[...] = jax.nn.sigmoid(logit * (1.0 / 4096.0))

    rest = ids_all.at[pl.ds(0, (CW - 1) * RW)]

    lane = iota((RW, 128), 1)
    base = (me * T).astype(F32)

    def wanted(row):
        table = jnp.full((RW, 128), -1.0, F32)
        for m in range(2):
            for i in range(RW):
                ids_flat[m, i : i + 1, :] = ids_all[row * RW + i, m : m + 1, :]
            local = ids_flat[m].astype(F32) - base
            inside = (local >= 0.0) & (local < float(T))
            first = jnp.min(jnp.where(inside, local, 1e6), axis=1, keepdims=True)
            last = jnp.max(jnp.where(inside, local, -1.0), axis=1, keepdims=True)
            first_ok = jnp.where(first < 1e5, first, -1.0)
            last_ok = jnp.where(last > first, last, -1.0)
            table = jnp.where(lane == 2 * m, first_ok, table)
            table = jnp.where(lane == 2 * m + 1, last_ok, table)
        return table

    here = pl.ds(pl.multiple_of(me * 16, 16), 16)

    def keep(src, dst, osem):
        own = pltpu.make_async_copy(src.at[here], dst.at[here], osem)
        own.start()
        return own

    def exchange(src, dst, ssem, rsem, begin_at, end_at):
        def one(k, carry):
            peer = lax.rem(me + k, E)
            pltpu.make_async_remote_copy(
                src_ref=src.at[pl.ds(pl.multiple_of(peer * 16, 16), 16)],
                dst_ref=dst.at[here],
                send_sem=ssem,
                recv_sem=rsem,
                device_id=(z, peer),
                device_id_type=MESH,
            ).start()
            return carry

        lax.fori_loop(begin_at, end_at, one, 0)

    def arrived(dst, rsem, own):
        own.wait()
        whole = dst.at[pl.ds(0, (E - 1) * 16)]
        pltpu.make_async_copy(whole, whole, rsem).wait()

    OB = RW * 16
    line = iota((OB, 1), 0)
    place = (((line // 4) % 4) * (2 * T) + ((line // 2) % 2) * T).astype(F32)
    spread = (line // 16 == iota((OB, RW), 1)).astype(F32)
    mine_lane = iota((OB, 128), 1) == iota((OB, 128), 0) % 4
    offsets = [sign * step for step in range(1, CW) for sign in (1, -1)][: CW - 1]
    offsets = [0] + offsets

    def send_row(offset, parity, src, dst, ssem, rsem):
        row = lax.rem(row_at + offset + CW, CW)

        def one(k, carry):
            peer = row * RW + lax.rem(col_at // 2 + k, RW // 2) * 2 + parity
            pltpu.make_async_remote_copy(
                src_ref=src.at[pl.ds(pl.multiple_of(peer * 16, 16), 16)],
                dst_ref=dst.at[here],
                send_sem=ssem,
                recv_sem=rsem,
                device_id=(z, peer),
                device_id_type=MESH,
            ).start()
            return carry

        own = jnp.where(lax.rem(col_at, 2) == parity, 1, 0) if offset == 0 else 0
        lax.fori_loop(own, RW // 2, one, 0)

    pltpu.make_async_copy(xcat, xcat, in_sem.at[2]).wait()
    for offset in offsets:
        row = lax.rem(row_at + offset + CW, CW)
        rows = pl.ds(pl.multiple_of(row * OB, OB), OB)
        if offset:
            theirs = ids_all.at[pl.ds(row * RW, RW)]
            pltpu.make_async_copy(theirs, theirs, ids_rsem.at[1 + row]).wait()
        values = jnp.dot(spread, wanted(row), preferred_element_type=F32)
        chosen = jnp.sum(jnp.where(mine_lane, values, 0.0), axis=1, keepdims=True)
        target = jnp.where(chosen < 0.0, -1.0, chosen + place)
        hot = (iota((OB, 8 * T), 1).astype(F32) == target).astype(F32).astype(BF16)
        onehot[rows, :] = hot
        send_x[rows, :] = jnp.dot(hot, xcat[...], preferred_element_type=F32).astype(BF16)
        send_row(offset, 0, send_x, got_x, fwd_ssem.at[0], fwd_rsem.at[0])
    own_x = keep(send_x, got_x, own_sem.at[0])
    pltpu.make_async_copy(gcat, gcat, in_sem.at[3]).wait()
    for offset in offsets:
        row = lax.rem(row_at + offset + CW, CW)
        rows = pl.ds(pl.multiple_of(row * OB, OB), OB)
        send_g[rows, :] = jnp.dot(
            onehot[rows, :], gcat[...], preferred_element_type=F32
        ).astype(BF16)
        send_row(offset, 0, send_g, got_g, fwd_ssem.at[1], fwd_rsem.at[1])
    for offset in offsets:
        send_row(offset, 1, send_x, got_x, fwd_ssem.at[0], fwd_rsem.at[0])
    for offset in offsets:
        send_row(offset, 1, send_g, got_g, fwd_ssem.at[1], fwd_rsem.at[1])
    own_g = keep(send_g, got_g, own_sem.at[1])

    r = iota((BR, BR), 0)
    c = iota((BR, BR), 1)
    perm = (
        c == ((r // 4) % BP) * 16 + (r // BO) * 4 + r % 4
    ).astype(F32).astype(BF16)
    perm_t = (
        r == ((c // 4) % BP) * 16 + (c // BO) * 4 + c % 4
    ).astype(F32).astype(BF16)

    for copy in weights:
        copy.wait()
    arrived(got_x, fwd_rsem.at[0], own_x)
    for blk in range(NB):
        moved = jnp.dot(perm, got_x[blk * BR : (blk + 1) * BR, :], preferred_element_type=F32)
        for q in range(4):
            xs[blk * BO : (blk + 1) * BO, q * Q : (q + 1) * Q] = moved[
                q * BO : (q + 1) * BO
            ].astype(BF16)
    FT = min(256, F)
    for ft in range(F // FT):
        cols = slice(ft * FT, (ft + 1) * FT)
        h1 = jnp.dot(xs[...], wg[:, cols], preferred_element_type=F32)
        h3 = jnp.dot(xs[...], wu[:, cols], preferred_element_type=F32)
        sig = jax.nn.sigmoid(h1)
        gated = h1 * sig
        act_t[cols, :] = (gated * h3).astype(BF16).T
        coef3[:, cols] = gated
        coef1[:, cols] = h3 * sig * (1.0 + h1 * (1.0 - sig))
    for q in range(4):
        xs_t[q * Q : (q + 1) * Q, :] = xs[:, q * Q : (q + 1) * Q].T

    arrived(got_g, fwd_rsem.at[1], own_g)
    for blk in range(NB):
        moved = jnp.dot(perm, got_g[blk * BR : (blk + 1) * BR, :], preferred_element_type=F32)
        scale = gates[blk * BO : (blk + 1) * BO, :]
        for q in range(4):
            dy[blk * BO : (blk + 1) * BO, q * Q : (q + 1) * Q] = (
                moved[q * BO : (q + 1) * BO] * scale
            ).astype(BF16)

    parts = (part_g, part_u, part_d0, part_d1)
    rings = (ring_g, ring_u, ring_d0, ring_d1)
    heights = (D // G, D // G, F // G, F // G)
    starts = ((0, 1, 0, 1), (1, 0, 1, 0))

    def piece(p, chunk):
        return pl.ds(pl.multiple_of(chunk * heights[p], heights[p]), heights[p])

    def forward(way, p, step, src):
        pltpu.make_async_remote_copy(
            src_ref=src,
            dst_ref=rings[p].at[way, step],
            send_sem=ring_ssem.at[way, p, step],
            recv_sem=ring_rsem.at[way, p, step],
            device_id=(z_right if way == 0 else z_left, me),
            device_id_type=MESH,
        ).start()

    def ring_copy(way, p, step):
        return pltpu.make_async_remote_copy(
            src_ref=rings[p].at[way, step],
            dst_ref=rings[p].at[way, step],
            send_sem=ring_ssem.at[way, p, step],
            recv_sem=ring_rsem.at[way, p, step],
            device_id=(z_right if way == 0 else z_left, me),
            device_id_type=MESH,
        )

    far = lax.rem(z + S, G)

    def begin(p):
        forward(starts[0][p], p, 0, parts[p].at[piece(p, far)])

    for ft in range(F // FT):
        rows = slice(ft * FT, (ft + 1) * FT)
        for half, part in ((0, part_d0), (1, part_d1)):
            part[rows, :] = (
                jnp.dot(
                    act_t[rows, :],
                    dy[:, half * (D // 2) : (half + 1) * (D // 2)],
                    preferred_element_type=F32,
                )
                * factor
            ).astype(BF16)
    begin(2)
    begin(3)
    for ft in range(F // FT):
        cols = slice(ft * FT, (ft + 1) * FT)
        dact = lax.dot_general(dy[...], wd[cols, :], contract_cols, preferred_element_type=F32)
        dh1[:, cols] = (dact * coef1[:, cols]).astype(BF16)
        dh3[:, cols] = (dact * coef3[:, cols]).astype(BF16)
    for p, part, dh in ((0, part_g, dh1), (1, part_u, dh3)):
        for q in range(4):
            rows = slice(q * Q, (q + 1) * Q)
            part[rows, :] = (
                jnp.dot(xs_t[rows, :], dh[...], preferred_element_type=F32) * factor
            ).astype(BF16)
        begin(p)

    def chunk_at(way, step):
        if way == 0:
            return lax.rem(z + S - step + G, G)
        return lax.rem(z + S + step, G)

    def pass_on(way, p, step):
        ring_copy(way, p, step - 1).wait_recv()
        held = rings[p].at[way, step - 1]
        held[...] = (
            held[...].astype(F32) + parts[p][piece(p, chunk_at(way, step)), :].astype(F32)
        ).astype(BF16)
        forward(way, p, step, held)

    order = ((0, 2), (1, 3), (0, 0), (1, 1), (0, 3), (1, 2), (0, 1), (1, 0))
    for way, p in order:
        if starts[way][p] == 1:
            forward(way, p, 1, parts[p].at[piece(p, chunk_at(way, 1))])
    for way, p in order:
        if starts[way][p] == 0:
            pass_on(way, p, 1)

    for q in range(4):
        rows = slice(q * Q, (q + 1) * Q)
        dx = (
            lax.dot_general(dh1[...], wg[rows, :], contract_cols, preferred_element_type=F32)
            + lax.dot_general(dh3[...], wu[rows, :], contract_cols, preferred_element_type=F32)
        ).astype(BF16)
        for blk in range(NB):
            dx_cat[blk * BR + q * BO : blk * BR + (q + 1) * BO, :] = dx[blk * BO : (blk + 1) * BO]
    for blk in range(NB):
        rows = slice(blk * BR, (blk + 1) * BR)
        send_r[rows, :] = jnp.dot(
            perm_t, dx_cat[rows, :], preferred_element_type=F32
        ).astype(BF16)
    turns = max(S - 4, 1)
    per = -(-(E - 1) // turns)
    exchange(send_r, got_r, ret_ssem, ret_rsem, 1, min(1 + per, E))
    own_r = keep(send_r, got_r, own_sem.at[2])

    def ring_step(step, carry):
        for way, p in order:
            pass_on(way, p, step)
        begin_at = jnp.minimum(1 + (step - 1) * per, E)
        end_at = jnp.minimum(begin_at + per, E)
        exchange(send_r, got_r, ret_ssem, ret_rsem, begin_at, end_at)
        return carry

    lax.fori_loop(2, S, ring_step, 0)

    arrived(got_r, ret_rsem, own_r)
    summed = lax.dot_general(onehot[...], got_r[...], contract_rows, preferred_element_type=F32)
    for m in range(2):
        for q in range(4):
            tok_ref[m, :, q * Q : (q + 1) * Q] = summed[
                (q * 2 + m) * T : (q * 2 + m + 1) * T
            ].astype(BF16)

    def finish(p):
        ring_copy(0, p, S - 1).wait_recv()
        ring_copy(1, p, S - 1).wait_recv()
        return (
            rings[p][0, S - 1].astype(F32)
            + rings[p][1, S - 1].astype(F32)
            + parts[p][piece(p, z), :].astype(F32)
        ).astype(BF16)

    down_ref[0, :, 0 : D // 2] = finish(2)
    down_ref[0, :, D // 2 : D] = finish(3)
    gate_ref[0] = finish(0)
    up_ref[0] = finish(1)

    if RW > 1:
        pltpu.make_async_copy(near, near, ids_ssem.at[0]).wait()
    pltpu.make_async_copy(rest, rest, ids_ssem.at[1]).wait()
    for src, sem in ((send_x, fwd_ssem.at[0]), (send_g, fwd_ssem.at[1]), (send_r, ret_ssem)):
        whole = src.at[pl.ds(0, (E - 1) * 16)]
        pltpu.make_async_copy(whole, whole, sem).wait()
    for way in range(2):
        for p in range(4):
            for step in range(starts[way][p], S):
                ring_copy(way, p, step).wait_send()


def settle(*refs):
    number = len(refs) // 2
    sems = refs[-1]
    copies = [
        pltpu.make_async_copy(refs[k], refs[number + k], sems.at[k]) for k in range(number)
    ]
    for copy in copies:
        copy.start()
    for copy in copies:
        copy.wait()


def body(activations, out_grads, chosen_ids, gate_logits, w_gate, w_up, w_down):
    E = lax.axis_size("expert")
    G = lax.axis_size("dp")
    T, D = activations.shape[1:]
    F = w_gate.shape[-1]
    C = chosen_ids.shape[-1]
    Q, S, R4, R16 = D // 4, G // 2, 4 * E, 16 * E
    RW = min(8, E // 2)
    vmem = pl.BlockSpec(memory_space=pltpu.VMEM)
    hbm = pl.BlockSpec(memory_space=pltpu.HBM)
    V = pltpu.VMEM
    dma = pltpu.SemaphoreType.DMA
    scratch = [
        V((2, 1, 1, C), jnp.int32), V((2, 1, 1, C), jnp.int32),
        V((2, 128), jnp.int32), V((2, 128), jnp.int32),
        V((E, 2, 128), jnp.int32), V((2, RW, 128), jnp.int32),
        V((D, F), BF16), V((D, F), BF16), V((F, D), BF16),
        V((8 * T, Q), BF16), V((8 * T, Q), BF16), V((R16, 8 * T), BF16),
        V((R16, Q), BF16), V((R16, Q), BF16), V((R16, Q), BF16), V((R16, Q), BF16),
        V((R4, D), BF16), V((D, R4), BF16), V((R4, D), BF16), V((F, R4), BF16),
        V((R4, F), F32), V((R4, F), F32), V((R4, F), BF16), V((R4, F), BF16), V((R4, 1), F32),
        V((R16, Q), BF16), V((R16, Q), BF16), V((R16, Q), BF16),
        V((D, F), BF16), V((D, F), BF16), V((F, D // 2), BF16), V((F, D // 2), BF16),
        V((2, S, D // G, F), BF16), V((2, S, D // G, F), BF16),
        V((2, S, F // G, D // 2), BF16), V((2, S, F // G, D // 2), BF16),
        dma((3,)), dma((4,)), dma((2,)), dma((1 + E // RW,)), dma((2,)), dma((2,)), dma((3,)), dma, dma,
        dma((2, 4, S)), dma((2, 4, S)),
    ]
    shape = jax.ShapeDtypeStruct
    results = pl.pallas_call(
        functools.partial(fused, (E, G, T, D, F, C)),
        out_shape=(
            shape((2, T, D), BF16),
            shape((1, D // G, F), BF16),
            shape((1, D // G, F), BF16),
            shape((1, F // G, D), BF16),
        ),
        in_specs=[hbm] * 7,
        out_specs=(vmem, vmem, vmem, vmem),
        scratch_shapes=scratch,
        compiler_params=pltpu.CompilerParams(
            collective_id=0, has_side_effects=True, vmem_limit_bytes=533 * 1024 * 1024 // 10
        ),
    )(chosen_ids, gate_logits, activations, out_grads, w_gate, w_up, w_down)
    return pl.pallas_call(
        settle,
        out_shape=tuple(shape(item.shape, item.dtype) for item in results),
        in_specs=[vmem] * 4,
        out_specs=(hbm,) * 4,
        scratch_shapes=[dma((4,))],
        compiler_params=pltpu.CompilerParams(vmem_limit_bytes=16 * 1024 * 1024),
    )(*results)


def solution(mesh):
    placed = (
        P(None, ("dp", "expert"), None),
        P(None, ("dp", "expert"), None),
        P(None, "dp", "expert", None),
        P(None, "dp", "expert", None),
        P("expert", None, None),
        P("expert", None, None),
        P("expert", None, None),
    )
    return jax.shard_map(
        body,
        mesh=mesh,
        in_specs=placed,
        out_specs=(
            P(None, ("dp", "expert"), None),
            P("expert", "dp", None),
            P("expert", "dp", None),
            P("expert", "dp", None),
        ),
        check_vma=False,
    )
```
